128 devices in a mesh: row: 8 (over y, core), col: 16 (over z, x).
Axes of the slice: x: 4, y: 4, z: 4, core: 2. Of those that a mesh axis runs over, the one named last changes fastest.
Arguments:
- orbital_blocks: bfloat16 [768, 256, 1024], P(('row', 'col')), may hold values from -1.1953125 to 1.1953125
- orbital_slot: int32 [768], replicated, may hold values from 0 to 767, as said below
- pair_first: int32 [4096], P(('row', 'col')), may hold values from 0 to 767, as said below
- pair_second: int32 [4096], P(('row', 'col')), may hold values from 0 to 767, as said below
- occupied_energy: float32 [768], replicated, may hold values from -1 to 0
- virtual_energy: float32 [256], replicated, may hold values from 0.25 to 1
Outputs:
- block_gradient: float32 [768, 256, 1024], P(('row', 'col'))
The draws below stay inside these ranges and needn't reach their ends.
Inputs may be any that keep to these rules, and one draw needn't show every extreme that they name: `orbital_slot`: A permutation: every storage position holds exactly one orbital. `pair_first`: with device d = r * 16 + c handling pairs d * 32 to (d + 1) * 32 - 1 and position p stored on device p // 6: each first orbital is stored on a device of column c; among one device's pairs at most 2 distinct first orbitals are stored on any one device, and in every draw each device has exactly 2 from some device. The pairs (first, second) of a device are distinct. `pair_second`: each second orbital is stored on a device of the pair device's row r; among one device's pairs at most 1 distinct second orbitals are stored on any one device.
All inputs are finite; a program needn't handle non-finite values.
Results may differ from the reference program's by a relative error of at most 0.0025.
Values may be sent and summed in bfloat16 or wider, within the bound.
A program may use at most 192 MiB of HBM per device.

```python
import jax
import jax.numpy as jnp
from jax import lax

V = 256
NAUX = 1024
ORB_DEV = 6
PAIR_DEV = 32
ORBITALS = 768
N_ROW = 8
N_COL = 16
DEVICES = 128


def pair_tables(key):
    devices = N_ROW * N_COL
    at_position = jax.random.permutation(jax.random.fold_in(key, 101), ORBITALS)
    slot_table = jnp.zeros((ORBITALS,), jnp.int32).at[at_position].set(jnp.arange(ORBITALS, dtype=jnp.int32))
    dev_rows = jnp.arange(devices) // N_COL
    dev_cols = jnp.arange(devices) % N_COL
    icount = jax.random.randint(jax.random.fold_in(key, 102), (devices, N_ROW), 1, 3)
    forced = jax.random.randint(jax.random.fold_in(key, 103), (devices,), 0, N_ROW)
    icount = jnp.where(jnp.arange(N_ROW)[None, :] == forced[:, None], 2, icount)
    local_one = jax.random.randint(jax.random.fold_in(key, 104), (devices, N_ROW), 0, ORB_DEV)
    local_two = (local_one + jax.random.randint(jax.random.fold_in(key, 105), (devices, N_ROW), 1, ORB_DEV)) % ORB_DEV
    ilocal = jnp.stack([local_one, local_two], axis=-1)
    isource = jnp.arange(N_ROW)[None, :] * N_COL + dev_cols[:, None]
    ipos = (isource[:, :, None] * ORB_DEV + ilocal).reshape(devices, 2 * N_ROW)
    ivalid = (jnp.arange(2)[None, None, :] < icount[:, :, None]).reshape(devices, 2 * N_ROW)
    jshift = jax.random.randint(jax.random.fold_in(key, 106), (devices,), 0, N_COL)
    jbase = jax.random.randint(jax.random.fold_in(key, 107), (devices, N_COL), 0, 2)
    jvalid = ((jnp.arange(N_COL)[None, :] - jshift[:, None]) % N_COL < 4) | (jbase == 1)
    jlocal = jax.random.randint(jax.random.fold_in(key, 108), (devices, N_COL), 0, ORB_DEV)
    jsource = dev_rows[:, None] * N_COL + jnp.arange(N_COL)[None, :]
    jpos = jsource * ORB_DEV + jlocal
    combos = 2 * N_ROW * N_COL
    keys = jax.random.split(jax.random.fold_in(key, 109), devices)
    scores = jax.vmap(lambda k: jax.random.permutation(k, combos))(keys) + 2
    upper = jnp.arange(combos)[None, :] // N_COL
    lower = jnp.arange(combos)[None, :] % N_COL
    valid = jnp.take_along_axis(ivalid, upper + 0 * scores, axis=1) & jnp.take_along_axis(jvalid, lower + 0 * scores, axis=1)
    scores = jnp.where(valid, scores, scores + combos + 2)
    priority = (upper // 2 == forced[:, None]) & (lower == jshift[:, None])
    scores = jnp.where(priority, upper % 2, scores)
    order = jnp.argsort(scores, axis=1, stable=True)[:, :PAIR_DEV]
    first_pos = jnp.take_along_axis(ipos, order // N_COL, axis=1)
    second_pos = jnp.take_along_axis(jpos, order % N_COL, axis=1)
    first = at_position[first_pos.reshape(-1)].astype(jnp.int32)
    second = at_position[second_pos.reshape(-1)].astype(jnp.int32)
    return (slot_table, first, second)


def draw_orbital_slot(key, part):
    tables = pair_tables(key)
    return tables[0]


def draw_pair_first(key, part):
    tables = pair_tables(key)
    return tables[1]


def draw_pair_second(key, part):
    tables = pair_tables(key)
    return tables[2]


def levels(own_key, shape, shards, smallest, largest):
    gain, own = 1.0, jax.random.fold_in(own_key, 6)
    for dim, shards_of in shards:
        draws = jnp.exp(jax.random.uniform(jax.random.fold_in(own, dim), (shards_of,), jnp.float32, smallest / len(shards), largest / len(shards)))
        gain = gain * jnp.repeat(draws, shape[dim] // shards_of).reshape([-1 if axis == dim else 1 for axis in range(len(shape))])
    return gain


def normal_values(key, dims, spread, most, shards=(), held_as=jnp.bfloat16):
    factor_of = levels(key, dims, shards, -0.22, 0.18) if shards else 1.0
    drawn = jax.random.normal(key, dims, jnp.float32) * spread * factor_of
    return jnp.minimum(jnp.maximum(drawn, -most), most).astype(held_as)


def setup_inputs(seed: int = 0) -> dict:
    key_of = jax.random.split(jax.random.key(seed), 7)
    return {
        "orbital_blocks": normal_values(key_of[0], (ORBITALS, V, NAUX), 0.18, 1.1953125, ((0, 128),)),
        "orbital_slot": draw_orbital_slot(jax.random.fold_in(key_of[6], 71), 0),
        "pair_first": draw_pair_first(jax.random.fold_in(key_of[6], 71), 0),
        "pair_second": draw_pair_second(jax.random.fold_in(key_of[6], 71), 0),
        "occupied_energy": jnp.clip(jax.random.uniform(key_of[4], (ORBITALS,), jnp.float32, -1.0, 0.0), -1.0, 0.0),
        "virtual_energy": jnp.clip(jax.random.uniform(key_of[5], (V,), jnp.float32, 0.25, 1.0), 0.25, 1.0),
    }


def leaders(positions):
    count = positions.shape[0]
    order = jnp.arange(count)
    same = positions[:, None] == positions[None, :]
    earlier = same & (order[None, :] < order[:, None])
    return jnp.logical_not(jnp.any(earlier, axis=1)), same


def reference(orbital_blocks, orbital_slot, pair_first, pair_second, occupied_energy, virtual_energy):
    first_pos = orbital_slot[pair_first].reshape(DEVICES, PAIR_DEV)
    second_pos = orbital_slot[pair_second].reshape(DEVICES, PAIR_DEV)
    pair_energy = (occupied_energy[pair_first] + occupied_energy[pair_second]).reshape(DEVICES, PAIR_DEV)
    virtual_sum = virtual_energy[:, None] + virtual_energy[None, :]

    def step(grads, inputs):
        fpos, spos, occ = inputs
        left_blocks = orbital_blocks[fpos].astype(jnp.float32)
        right_blocks = orbital_blocks[spos].astype(jnp.float32)
        integrals = jnp.einsum("pax,pbx->pab", left_blocks, right_blocks)
        den = virtual_sum[None, :, :] - occ[:, None, None]
        amplitudes = integrals / den
        weights = (2.0 * amplitudes - jnp.swapaxes(amplitudes, 1, 2)).astype(jnp.bfloat16).astype(jnp.float32)
        left_terms = jnp.einsum("pab,pbx->pax", weights, right_blocks)
        right_terms = jnp.einsum("pab,pax->pbx", weights, left_blocks)
        lead_first, same_first = leaders(fpos)
        lead_second, same_second = leaders(spos)
        first_sums = jnp.einsum("pq,qax->pax", same_first.astype(jnp.float32), left_terms)
        second_sums = jnp.einsum("pq,qax->pax", same_second.astype(jnp.float32), right_terms)
        first_sums = first_sums.astype(jnp.bfloat16).astype(jnp.float32)
        second_sums = second_sums.astype(jnp.bfloat16).astype(jnp.float32)
        first_sums = jnp.where(lead_first[:, None, None], first_sums, jnp.float32(0.0))
        second_sums = jnp.where(lead_second[:, None, None], second_sums, jnp.float32(0.0))
        grads = grads.at[fpos].add(first_sums)
        grads = grads.at[spos].add(second_sums)
        return grads, None

    start = jnp.zeros((ORBITALS, V, NAUX), jnp.float32)
    grads, _ = lax.scan(step, start, (first_pos, second_pos, pair_energy))
    return grads
```

```python
import functools

import jax
import jax.numpy as jnp
from jax import lax
from jax.experimental import pallas as pl
from jax.experimental.pallas import tpu as pltpu
from jax.sharding import PartitionSpec as P

MESH = pl.DeviceIdType.MESH
I_CAP = 2
CHUNK = 256
HALF = 128
FS, SS, KF, OS, KS, LF, LS = 0, 32, 64, 96, 128, 160, 176
TABLE = 192
NONE = 7


def places(n_row, n_col):
    row = lax.axis_index("row")
    col = lax.axis_index("col")
    return row, col


def row_step(row, e, sign):
    y = (row // 2 + sign * (e // 2) + 4) % 4
    k = (row % 2 + e % 2) % 2
    return y * 2 + k


def col_step(col, e, sign):
    z = (col // 4 + sign * (e // 4) + 4) % 4
    x = (col % 4 + sign * (e % 4) + 4) % 4
    return z * 4 + x


def plan_kernel(
    orb_dev, n_row, n_col, slot, first, second, occ, table, energy, request, key_f, key_s, at_f, at_s, place
):
    row, col = places(n_row, n_col)
    pairs = first.shape[0]
    shift = 16
    magic = (1 << shift) // orb_dev + 1

    def clear(i, carry):
        at_f[i] = 0
        at_s[i] = 0
        at_s[i + n_row * 8] = 0
        return carry

    lax.fori_loop(0, n_row * 8, clear, 0)

    def count(p, carry):
        i = first[p]
        j = second[p]
        energy[p] = occ[i] + occ[j]
        pos_i = slot[i]
        pos_j = slot[j]
        dev_i = (pos_i * magic) >> shift
        dev_j = (pos_j * magic) >> shift
        row_i = dev_i >> 4
        col_j = dev_j & 15
        e_i = ((((row >> 1) - (row_i >> 1)) & 3) << 1) | ((row ^ row_i) & 1)
        e_j = ((((col >> 2) - (col_j >> 2)) & 3) << 2) | ((col - col_j) & 3)
        f = e_i * 8 + pos_i - dev_i * orb_dev
        s = e_j * 8 + pos_j - dev_j * orb_dev
        key_f[p] = f
        key_s[p] = s
        at_f[f] = at_f[f] + 1
        at_s[s] = at_s[s] + 1
        return carry

    lax.fori_loop(0, pairs, count, 0)

    def rank_f(e, start):
        ask = NONE + 8 * NONE
        found = 0
        table[LF + e * I_CAP + 1] = 0
        for local in range(orb_dev):
            here = at_f[e * 8 + local]
            at_f[e * 8 + local] = start
            some = here > 0
            ask = jnp.where(some, jnp.where(found == 0, local + 8 * NONE, (ask & 7) + 8 * local), ask)
            place[e * 8 + local] = e * I_CAP + jnp.minimum(found, I_CAP - 1)
            start = start + here
            table[LF + e * I_CAP + jnp.minimum(found, I_CAP - 1)] = jnp.maximum(start - 1, 0)
            found = found + some.astype(jnp.int32)
        request[e, 0] = ask
        return start

    lax.fori_loop(0, n_row, rank_f, 0)

    def rank_s(e, start):
        ask = NONE
        for local in range(orb_dev):
            here = at_s[e * 8 + local]
            at_s[e * 8 + local] = start
            ask = jnp.where(here > 0, local, ask)
            start = start + here
        table[LS + e] = jnp.maximum(start - 1, 0)
        request[n_row + e, 0] = ask
        return start

    lax.fori_loop(0, n_col, rank_s, 0)

    def order_f(p, carry):
        f = key_f[p]
        q = at_f[f]
        at_f[f] = q + 1
        table[FS + q] = place[f]
        table[SS + q] = key_s[p] >> 3
        table[KS + q] = key_s[p]
        place[n_row * 8 + q] = p
        return carry

    lax.fori_loop(0, pairs, order_f, 0)

    def order_s(q, carry):
        s = table[KS + q]
        at = at_s[s]
        at_s[s] = at + 1
        table[OS + at] = q
        return carry

    lax.fori_loop(0, pairs, order_s, 0)

    def keep(q, carry):
        before = jnp.maximum(q - 1, 0)
        same_f = (table[FS + q] == table[FS + before]) & (q > 0)
        same_s = (table[SS + table[OS + q]] == table[SS + table[OS + before]]) & (q > 0)
        table[KF + q] = same_f.astype(jnp.int32)
        table[KS + q] = same_s.astype(jnp.int32)
        key_f[q] = place[n_row * 8 + q]
        return carry

    lax.fori_loop(0, pairs, keep, 0)

    def energies(p, carry):
        q = key_f[p]
        energy[pairs + p] = energy[q]
        return carry

    lax.fori_loop(0, pairs, energies, 0)


def pair_kernel(
    n_row,
    n_col,
    table,
    energy,
    request,
    blocks,
    energy_col,
    energy_row,
    back,
    asked,
    send_l,
    send_r,
    recv_l,
    recv_r,
    mat,
    weight,
    weight_t,
    ask_send,
    ask_recv,
    out_sem,
    in_sem,
    own_sem,
):
    row, col = places(n_row, n_col)
    fitting = blocks.shape[2]
    pairs = mat.shape[0]
    chunks = fitting // CHUNK
    slots_f = n_row * I_CAP
    virtuals = blocks.shape[1]
    halves = virtuals // HALF

    def to_row(e):
        return (row_step(row, e, 1), col)

    def to_col(e):
        return (row, col_step(col, e, 1))

    def from_row(e):
        return (row_step(row, e, -1), col)

    def from_col(e):
        return (row, col_step(col, e, -1))

    barrier = pltpu.get_barrier_semaphore()

    def greet(e, carry):
        pl.semaphore_signal(barrier, inc=1, device_id=to_col(e), device_id_type=MESH)

        @pl.when(e < n_row)
        def _():
            pl.semaphore_signal(barrier, inc=1, device_id=to_row(e), device_id_type=MESH)

        return carry

    lax.fori_loop(1, n_col, greet, 0)
    pl.semaphore_wait(barrier, n_row + n_col - 2)

    def ask_copy(slot, target):
        return pltpu.make_async_remote_copy(
            src_ref=request.at[slot],
            dst_ref=asked.at[slot],
            send_sem=ask_send.at[slot],
            recv_sem=ask_recv.at[slot],
            device_id=target,
            device_id_type=MESH,
        )

    def ask(e, carry):
        ask_copy(n_row + e, from_col(e)).start()

        @pl.when(e < n_row)
        def _():
            ask_copy(e, from_row(e)).start()

        return carry

    lax.fori_loop(1, n_col, ask, 0)
    asked[0, 0] = request[0, 0]
    asked[n_row, 0] = request[n_row, 0]

    def ask_wait(e, carry):
        ask_copy(n_row + e, from_col(e)).wait()

        @pl.when(e < n_row)
        def _():
            ask_copy(e, from_row(e)).wait()

        return carry

    lax.fori_loop(1, n_col, ask_wait, 0)

    def local_of(code):
        return jnp.where(code == NONE, 0, code)

    def copy_l(k, h, e):
        part = pl.ds(h * HALF, HALF)
        place = pl.ds(e * I_CAP, I_CAP)
        return pltpu.make_async_remote_copy(
            src_ref=send_l.at[k, place, part],
            dst_ref=recv_l[k].at[place, part],
            send_sem=out_sem.at[0, k],
            recv_sem=in_sem.at[0, k],
            device_id=to_row(e),
            device_id_type=MESH,
        )

    def copy_r(k, h, e):
        part = pl.ds(h * HALF, HALF)
        return pltpu.make_async_remote_copy(
            src_ref=send_r.at[k, e, part],
            dst_ref=recv_r[k].at[e, part],
            send_sem=out_sem.at[1, k],
            recv_sem=in_sem.at[1, k],
            device_id=to_col(e),
            device_id_type=MESH,
        )

    for k in range(chunks):
        columns = slice(k * CHUNK, (k + 1) * CHUNK)

        def forward(e, carry):
            send_r[k, e] = blocks[local_of(asked[n_row + e, 0]), :, columns]
            copy_r(k, 0, e).start()

            @pl.when(e < n_row)
            def _():
                code = asked[e, 0]
                send_l[k, e * I_CAP] = blocks[local_of(code & 7), :, columns]
                send_l[k, e * I_CAP + 1] = blocks[local_of(code >> 3), :, columns]
                copy_l(k, 0, e).start()

            return carry

        lax.fori_loop(1, n_col, forward, 0)

        def forward_rest(e, carry):
            for h in range(1, halves):
                copy_r(k, h, e).start()

                @pl.when(e < n_row)
                def _():
                    copy_l(k, h, e).start()

            return carry

        lax.fori_loop(1, n_col, forward_rest, 0)
        own = asked[0, 0]
        recv_l[k][0] = blocks[local_of(own & 7), :, columns]
        recv_l[k][1] = blocks[local_of(own >> 3), :, columns]
        recv_r[k][0] = blocks[local_of(asked[n_row, 0]), :, columns]

    for k in range(chunks):
        got_l = recv_l[k].at[pl.ds(I_CAP, slots_f - I_CAP)]
        got_r = recv_r[k].at[pl.ds(1, n_col - 1)]
        pltpu.make_async_copy(got_l, got_l, in_sem.at[0, k]).wait()
        pltpu.make_async_copy(got_r, got_r, in_sem.at[1, k]).wait()

        def integral(q, carry):
            left = recv_l[k][table[FS + q]]
            right = recv_r[k][table[SS + q]]
            part = lax.dot_general(
                left, right, (((1,), (1,)), ((), ())), preferred_element_type=jnp.float32
            )
            if k == 0:
                mat[q] = part
            else:
                mat[q] += part
            return carry

        lax.fori_loop(0, pairs, integral, 0)

    virtual_sum = energy_col[...] + energy_row[...]

    def weigh(q, carry):
        found = mat[q]
        turned = found.T
        scale = 1.0 / (virtual_sum - energy[pairs + q])
        weight[q] = ((2.0 * found - turned) * scale).astype(jnp.bfloat16)
        weight_t[q] = ((2.0 * turned - found) * scale).astype(jnp.bfloat16)
        return carry

    lax.fori_loop(0, pairs, weigh, 0)

    def back_l(k, h, e):
        part = pl.ds(h * HALF, HALF)
        place = pl.ds(e * I_CAP, I_CAP)
        return pltpu.make_async_remote_copy(
            src_ref=send_l.at[k, place, part],
            dst_ref=back.at[k, place, part],
            send_sem=out_sem.at[2, k],
            recv_sem=in_sem.at[2, k],
            device_id=from_row(e),
            device_id_type=MESH,
        )

    def back_r(k, h, e):
        part = pl.ds(h * HALF, HALF)
        return pltpu.make_async_remote_copy(
            src_ref=send_r.at[k, e, part],
            dst_ref=back.at[k, slots_f + e, part],
            send_sem=out_sem.at[3, k],
            recv_sem=in_sem.at[3, k],
            device_id=from_col(e),
            device_id_type=MESH,
        )

    def own_copies(k):
        return (
            pltpu.make_async_copy(send_l.at[k, pl.ds(0, I_CAP)], back.at[k, pl.ds(0, I_CAP)], own_sem.at[0, k]),
            pltpu.make_async_copy(send_r.at[k, 0], back.at[k, slots_f], own_sem.at[1, k]),
        )

    for k in range(chunks):
        sent_l = send_l.at[k, pl.ds(I_CAP, slots_f - I_CAP)]
        sent_r = send_r.at[k, pl.ds(1, n_col - 1)]
        pltpu.make_async_copy(sent_l, sent_l, out_sem.at[0, k]).wait()
        pltpu.make_async_copy(sent_r, sent_r, out_sem.at[1, k]).wait()

        def left_term(q, total):
            right = recv_r[k][table[SS + q]]
            term = jnp.dot(weight[q], right, preferred_element_type=jnp.float32)
            before = jnp.maximum(q - 1, 0)
            mat[q] = term + jnp.where(table[KF + q] > 0, mat[before], 0.0)
            return total

        lax.fori_loop(0, pairs, left_term, 0)

        def left_out(e, carry):
            for s in range(I_CAP):
                send_l[k, e * I_CAP + s] = mat[table[LF + e * I_CAP + s]].astype(jnp.bfloat16)

            @pl.when(e > 0)
            def _():
                for h in range(halves):
                    back_l(k, h, e).start()

            return carry

        lax.fori_loop(0, n_row, left_out, 0)

        def right_term(t, total):
            q = table[OS + t]
            left = recv_l[k][table[FS + q]]
            term = jnp.dot(weight_t[q], left, preferred_element_type=jnp.float32)
            before = jnp.maximum(t - 1, 0)
            mat[t] = term + jnp.where(table[KS + t] > 0, mat[before], 0.0)
            return total

        lax.fori_loop(0, pairs, right_term, 0)

        def right_out(e, carry):
            send_r[k, e] = mat[table[LS + e]].astype(jnp.bfloat16)

            @pl.when(e > 0)
            def _():
                for h in range(halves):
                    back_r(k, h, e).start()

            return carry

        lax.fori_loop(0, n_col, right_out, 0)
        for copy in own_copies(k):
            copy.start()

    for k in range(chunks):
        for copy in own_copies(k):
            copy.wait()
        sent_l = send_l.at[k, pl.ds(I_CAP, slots_f - I_CAP)]
        sent_r = send_r.at[k, pl.ds(1, n_col - 1)]
        pltpu.make_async_copy(sent_l, sent_l, out_sem.at[2, k]).wait()
        pltpu.make_async_copy(sent_r, sent_r, out_sem.at[3, k]).wait()
    for k in range(chunks):
        got_l = back.at[k, pl.ds(I_CAP, slots_f - I_CAP)]
        got_r = back.at[k, pl.ds(slots_f + 1, n_col - 1)]
        pltpu.make_async_copy(got_l, got_l, in_sem.at[2, k]).wait()
        pltpu.make_async_copy(got_r, got_r, in_sem.at[3, k]).wait()


def sum_kernel(n_row, n_col, asked, back, out, listed, counts):
    orb_dev = out.shape[0]
    chunks = back.shape[0]
    slots_f = n_row * I_CAP

    @pl.when(pl.program_id(0) == 0)
    def _():
        for o in range(8):
            counts[o] = 0

        def add(o, slot):
            at = counts[o]
            listed[o * 32 + at] = slot
            counts[o] = at + 1

        def firsts(e, carry):
            code = asked[e, 0]
            add(code & 7, e * I_CAP)
            add(code >> 3, e * I_CAP + 1)
            return carry

        lax.fori_loop(0, n_row, firsts, 0)

        def seconds(e, carry):
            add(asked[n_row + e, 0], slots_f + e)
            return carry

        lax.fori_loop(0, n_col, seconds, 0)

    for o in range(orb_dev):
        for k in range(chunks):

            def add_slot(i, total):
                return total + back[k, listed[o * 32 + i]].astype(jnp.float32)

            total = lax.fori_loop(0, counts[o], add_slot, jnp.zeros(back.shape[2:], jnp.float32))
            out[o, :, k * CHUNK : (k + 1) * CHUNK] = total


def shards(orbital_blocks, orbital_slot, pair_first, pair_second, occupied_energy, virtual_energy):
    n_row = lax.axis_size("row")
    n_col = lax.axis_size("col")
    orb_dev, virtuals, fitting = orbital_blocks.shape
    pairs = pair_first.shape[0]
    chunks = fitting // CHUNK
    slots_f = n_row * I_CAP
    slots = slots_f + n_col
    smem = pl.BlockSpec(memory_space=pltpu.SMEM)
    vmem = pl.BlockSpec(memory_space=pltpu.VMEM)
    table, energy, request = pl.pallas_call(
        functools.partial(plan_kernel, orb_dev, n_row, n_col),
        out_shape=(
            jax.ShapeDtypeStruct((TABLE,), jnp.int32),
            jax.ShapeDtypeStruct((2 * pairs,), jnp.float32),
            jax.ShapeDtypeStruct((n_row + n_col, 128), jnp.int32),
        ),
        in_specs=[smem] * 4,
        out_specs=(smem, smem, smem),
        scratch_shapes=[
            pltpu.SMEM((pairs,), jnp.int32),
            pltpu.SMEM((pairs,), jnp.int32),
            pltpu.SMEM((n_row * 8,), jnp.int32),
            pltpu.SMEM((n_col * 8,), jnp.int32),
            pltpu.SMEM((n_row * 8 + pairs,), jnp.int32),
        ],
    )(orbital_slot, pair_first, pair_second, occupied_energy)

    block = (virtuals, CHUNK)
    back, asked = pl.pallas_call(
        functools.partial(pair_kernel, n_row, n_col),
        out_shape=(
            jax.ShapeDtypeStruct((chunks, slots) + block, jnp.bfloat16),
            jax.ShapeDtypeStruct((n_row + n_col, 128), jnp.int32),
        ),
        in_specs=[smem, smem, smem, vmem, vmem, vmem],
        out_specs=(pl.BlockSpec(memory_space=pl.ANY), smem),
        scratch_shapes=[
            pltpu.VMEM((chunks, slots_f) + block, jnp.bfloat16),
            pltpu.VMEM((chunks, n_col) + block, jnp.bfloat16),
            [pltpu.VMEM((slots_f,) + block, jnp.bfloat16)] * chunks,
            [pltpu.VMEM((n_col,) + block, jnp.bfloat16)] * chunks,
            pltpu.VMEM((pairs, virtuals, virtuals), jnp.float32),
            pltpu.VMEM((pairs, virtuals, virtuals), jnp.bfloat16),
            pltpu.VMEM((pairs, virtuals, virtuals), jnp.bfloat16),
            pltpu.SemaphoreType.DMA((n_row + n_col,)),
            pltpu.SemaphoreType.DMA((n_row + n_col,)),
            pltpu.SemaphoreType.DMA((4, chunks)),
            pltpu.SemaphoreType.DMA((4, chunks)),
            pltpu.SemaphoreType.DMA((2, chunks)),
        ],
        compiler_params=pltpu.CompilerParams(
            collective_id=0, has_side_effects=True, vmem_limit_bytes=60 * 2**20
        ),
    )(
        table,
        energy,
        request,
        orbital_blocks,
        virtual_energy.reshape(virtuals, 1),
        virtual_energy.reshape(1, virtuals),
    )

    rows = 32
    return pl.pallas_call(
        functools.partial(sum_kernel, n_row, n_col),
        grid=(virtuals // rows,),
        out_shape=jax.ShapeDtypeStruct(orbital_blocks.shape, jnp.float32),
        in_specs=[smem, pl.BlockSpec((chunks, slots, rows, CHUNK), lambda i: (0, 0, i, 0))],
        out_specs=pl.BlockSpec((orb_dev, rows, fitting), lambda i: (0, i, 0)),
        scratch_shapes=[pltpu.SMEM((8 * 32,), jnp.int32), pltpu.SMEM((8,), jnp.int32)],
        compiler_params=pltpu.CompilerParams(vmem_limit_bytes=32 * 2**20),
    )(asked, back)


def solution(mesh):
    return jax.shard_map(
        shards,
        mesh=mesh,
        in_specs=(
            P(("row", "col"), None, None),
            P(),
            P(("row", "col")),
            P(("row", "col")),
            P(),
            P(),
        ),
        out_specs=P(("row", "col"), None, None),
        check_vma=False,
    )
```

```python
import functools

import jax
import jax.numpy as jnp
from jax import lax
from jax.experimental import pallas as pl
from jax.experimental.pallas import tpu as pltpu
from jax.sharding import PartitionSpec as P

MESH = pl.DeviceIdType.MESH
I_CAP = 2
PARTS = ((0, 256), (256, 256), (512, 256), (768, 128), (896, 128))
BACK_ORDER = (3, 0, 1, 2, 4)
PIECE = 128
NONE = 7
FAR = 1 << 20
UNROLL = 4
SUM_ROWS = 16
ASK, FS, SS, KF, OS, KS, LF, LS = range(8)


def row_step(row, e, sign):
    y = (row // 2 + sign * (e // 2) + 4) % 4
    k = (row % 2 + e % 2) % 2
    return y * 2 + k


def col_step(col, e, sign):
    z = (col // 4 + sign * (e // 4) + 4) % 4
    x = (col % 4 + sign * (e % 4) + 4) % 4
    return z * 4 + x


def plan(row, col, orb_dev, n_row, slot, first, second, occ, table, energy):
    pairs = first.shape[0]
    shape = (pairs, 128)
    lane = lax.broadcasted_iota(jnp.int32, shape, 1)
    sub = lax.broadcasted_iota(jnp.int32, shape, 0)
    shift = 16
    magic = (1 << shift) // orb_dev + 1

    def read(p, carry):
        f_down, f_across, s_down, s_across, e_down = carry
        i = first[p]
        j = second[p]
        pos_i = slot[i]
        pos_j = slot[j]
        dev_i = (pos_i * magic) >> shift
        dev_j = (pos_j * magic) >> shift
        row_i = dev_i >> 4
        col_j = dev_j & 15
        e_i = ((((row >> 1) - (row_i >> 1)) & 3) << 1) | ((row ^ row_i) & 1)
        e_j = ((((col >> 2) - (col_j >> 2)) & 3) << 2) | ((col - col_j) & 3)
        f = e_i * 8 + pos_i - dev_i * orb_dev
        s = e_j * 8 + pos_j - dev_j * orb_dev
        down = sub == p
        across = lane == p
        return (
            jnp.where(down, f, f_down),
            jnp.where(across, f, f_across),
            jnp.where(down, s, s_down),
            jnp.where(across, s, s_across),
            jnp.where(down, occ[i] + occ[j], e_down),
        )

    far = jnp.full(shape, FAR, jnp.int32)
    f_down, f_across, s_down, s_across, e_down = lax.fori_loop(
        0, pairs, read, (far, far, far, far, jnp.zeros(shape, jnp.float32)), unroll=8
    )

    def count(mask):
        return jnp.sum(mask.astype(jnp.int32), axis=1, keepdims=True)

    def line(values, keep):
        return jnp.sum(jnp.where(keep, values, jnp.zeros_like(values)), axis=0, keepdims=True)

    earlier = lane < sub
    same_f = f_across == f_down
    same_s = s_across == s_down
    rank_f = count((f_across < f_down) | (same_f & earlier))
    rank_s = count((s_across < s_down) | (same_s & earlier))
    behind = count(((f_across >> 3) == (f_down >> 3)) & (f_across < f_down)) > 0
    slot_f = (f_down >> 3) * I_CAP + behind.astype(jnp.int32)
    slot_s = s_down >> 3
    keep_f = (count(same_f & earlier) > 0).astype(jnp.int32) + jnp.zeros(shape, jnp.int32)
    keep_s = (count(same_s & earlier) > 0).astype(jnp.int32) + jnp.zeros(shape, jnp.int32)
    at_f = rank_f == lane
    at_s = rank_s == lane
    one = jnp.ones(shape, jnp.int32)
    mine_f = (f_down >> 3) == lane
    low = jnp.min(jnp.where(mine_f, f_down & 7, NONE), axis=0, keepdims=True)
    high = jnp.max(jnp.where(mine_f, f_down & 7, -1), axis=0, keepdims=True)
    ask_f = low + 8 * jnp.where(high > low, high, NONE)
    ask_s = jnp.min(jnp.where(slot_s == lane - n_row, s_down & 7, NONE), axis=0, keepdims=True)
    table[ASK : ASK + 1, :] = jnp.where(lane[:1] < n_row, ask_f, ask_s)
    table[FS : FS + 1, :] = line(slot_f, at_f)
    table[SS : SS + 1, :] = line(slot_s, at_f)
    table[KF : KF + 1, :] = line(keep_f, at_f)
    table[OS : OS + 1, :] = line(rank_f + jnp.zeros(shape, jnp.int32), at_s)
    table[KS : KS + 1, :] = line(keep_s, at_s)
    table[LF : LF + 1, :] = jnp.maximum(line(one, slot_f <= lane) - 1, 0)
    table[LS : LS + 1, :] = jnp.maximum(line(one, slot_s <= lane) - 1, 0)
    energy[0:1, :] = line(e_down, at_f)


def pair_kernel(
    n_row,
    n_col,
    slot,
    first,
    second,
    occ,
    energy_row,
    blocks_in,
    *refs,
):
    parts = len(PARTS)
    back = refs[:parts]
    part_sum, asked = refs[parts : parts + 2]
    (
        blocks,
        send_l,
        send_r,
        recv_l,
        recv_r,
        mat,
        weight,
        weight_t,
        table_v,
        energy_v,
        table,
        energy,
        pick,
        load_sem,
        ask_send,
        ask_recv,
        out_sem,
        in_sem,
        own_sem,
        sum_sem,
    ) = refs[parts + 2 :]
    row = lax.axis_index("row")
    col = lax.axis_index("col")
    orb_dev, virtuals, fitting = blocks.shape
    pairs = mat.shape[0]
    slots_f = n_row * I_CAP

    def to_row(e):
        return (row_step(row, e, 1), col)

    def to_col(e):
        return (row, col_step(col, e, 1))

    def from_row(e):
        return (row_step(row, e, -1), col)

    def from_col(e):
        return (row, col_step(col, e, -1))

    barrier = pltpu.get_barrier_semaphore()

    def greet(e, carry):
        pl.semaphore_signal(barrier, inc=1, device_id=to_col(e), device_id_type=MESH)

        @pl.when(e < n_row)
        def _():
            pl.semaphore_signal(barrier, inc=1, device_id=to_row(e), device_id_type=MESH)

        return carry

    lax.fori_loop(1, n_col, greet, 0)
    load = pltpu.make_async_copy(blocks_in, blocks, load_sem.at[0])
    load.start()
    plan(row, col, orb_dev, n_row, slot, first, second, occ, table_v, energy_v)
    to_scalar = (
        pltpu.make_async_copy(table_v, table, load_sem.at[1]),
        pltpu.make_async_copy(energy_v, energy, load_sem.at[2]),
    )
    for copy in to_scalar:
        copy.start()
    for copy in to_scalar:
        copy.wait()
    pl.semaphore_wait(barrier, n_row + n_col - 2)

    def ask_copy(place, target):
        return pltpu.make_async_remote_copy(
            src_ref=table.at[ASK],
            dst_ref=asked.at[place],
            send_sem=ask_send.at[place],
            recv_sem=ask_recv.at[place],
            device_id=target,
            device_id_type=MESH,
        )

    def ask(e, carry):
        ask_copy(n_row + e, from_col(e)).start()

        @pl.when(e < n_row)
        def _():
            ask_copy(e, from_row(e)).start()

        return carry

    lax.fori_loop(1, n_col, ask, 0)
    asked[0, 0] = table[ASK, 0]
    asked[n_row, n_row] = table[ASK, n_row]
    load.wait()

    def local_of(code):
        return jnp.where(code == NONE, 0, code)

    def copy_l(k, h, e):
        rows = pl.ds(h * PIECE, PIECE)
        place = pl.ds(e * I_CAP, I_CAP)
        return pltpu.make_async_remote_copy(
            src_ref=send_l[k].at[place, rows],
            dst_ref=recv_l[k].at[place, rows],
            send_sem=out_sem.at[0, k],
            recv_sem=in_sem.at[0, k],
            device_id=to_row(e),
            device_id_type=MESH,
        )

    def copy_r(k, h, e):
        rows = pl.ds(h * PIECE, PIECE)
        return pltpu.make_async_remote_copy(
            src_ref=send_r[k].at[e, rows],
            dst_ref=recv_r[k].at[e, rows],
            send_sem=out_sem.at[1, k],
            recv_sem=in_sem.at[1, k],
            device_id=to_col(e),
            device_id_type=MESH,
        )

    pieces = virtuals // PIECE
    for k, (start, width) in enumerate(PARTS):
        columns = slice(start, start + width)

        def forward(e, carry):
            if k == 0:
                ask_copy(n_row + e, from_col(e)).wait()
            send_r[k][e] = blocks[local_of(asked[n_row + e, n_row + e]), :, columns]
            copy_r(k, 0, e).start()

            @pl.when(e < n_row)
            def _():
                if k == 0:
                    ask_copy(e, from_row(e)).wait()
                code = asked[e, e]
                send_l[k][e * I_CAP] = blocks[local_of(code & 7), :, columns]
                send_l[k][e * I_CAP + 1] = blocks[local_of(code >> 3), :, columns]
                copy_l(k, 0, e).start()

            return carry

        lax.fori_loop(1, n_col, forward, 0)

        def forward_rest(e, carry):
            for h in range(1, pieces):
                copy_r(k, h, e).start()

                @pl.when(e < n_row)
                def _():
                    copy_l(k, h, e).start()

            return carry

        lax.fori_loop(1, n_col, forward_rest, 0)
        own = asked[0, 0]
        recv_l[k][0] = blocks[local_of(own & 7), :, columns]
        recv_l[k][1] = blocks[local_of(own >> 3), :, columns]
        recv_r[k][0] = blocks[local_of(asked[n_row, n_row]), :, columns]

    for o in range(orb_dev):

        def pick_first(e, carry):
            code = asked[e, e]
            found = jnp.where((code >> 3) == o, e * I_CAP + 1, -1)
            pick[o, e] = jnp.where((code & 7) == o, e * I_CAP, found)
            return carry

        def pick_second(e, carry):
            pick[o, n_row + e] = jnp.where(asked[n_row + e, n_row + e] == o, slots_f + e, -1)
            return carry

        lax.fori_loop(0, n_row, pick_first, 0)
        lax.fori_loop(0, n_col, pick_second, 0)

    virtual_row = jnp.broadcast_to(energy_row[...], (virtuals, virtuals))
    virtual_sum = virtual_row.T + virtual_row
    for k in range(parts):
        got_l = recv_l[k].at[pl.ds(I_CAP, slots_f - I_CAP)]
        got_r = recv_r[k].at[pl.ds(1, n_col - 1)]
        pltpu.make_async_copy(got_l, got_l, in_sem.at[0, k]).wait()
        pltpu.make_async_copy(got_r, got_r, in_sem.at[1, k]).wait()

        def integral(q, carry):
            left = recv_l[k][table[FS, q]]
            right = recv_r[k][table[SS, q]]
            found = lax.dot_general(
                left, right, (((1,), (1,)), ((), ())), preferred_element_type=jnp.float32
            )
            if k > 0:
                found = mat[q] + found
            if k < parts - 1:
                mat[q] = found
                return carry
            turned = found.T
            scale = 1.0 / (virtual_sum - energy[0, q])
            weight[q] = ((2.0 * found - turned) * scale).astype(jnp.bfloat16)
            weight_t[q] = ((2.0 * turned - found) * scale).astype(jnp.bfloat16)
            return carry

        lax.fori_loop(0, pairs, integral, 0, unroll=UNROLL)

    def back_l(k, h, e):
        rows = pl.ds(h * PIECE, PIECE)
        place = pl.ds(e * I_CAP, I_CAP)
        return pltpu.make_async_remote_copy(
            src_ref=send_l[k].at[place, rows],
            dst_ref=back[k].at[place, rows],
            send_sem=out_sem.at[2, k],
            recv_sem=in_sem.at[2, k],
            device_id=from_row(e),
            device_id_type=MESH,
        )

    def back_r(k, h, e):
        rows = pl.ds(h * PIECE, PIECE)
        return pltpu.make_async_remote_copy(
            src_ref=send_r[k].at[e, rows],
            dst_ref=back[k].at[slots_f + e, rows],
            send_sem=out_sem.at[3, k],
            recv_sem=in_sem.at[3, k],
            device_id=from_col(e),
            device_id_type=MESH,
        )

    def own_copies(k):
        own = pl.ds(0, I_CAP)
        return (
            pltpu.make_async_copy(send_l[k].at[own], back[k].at[own], own_sem.at[0, k]),
            pltpu.make_async_copy(send_r[k].at[0], back[k].at[slots_f], own_sem.at[1, k]),
        )

    def sent(k):
        return send_l[k].at[pl.ds(I_CAP, slots_f - I_CAP)], send_r[k].at[pl.ds(1, n_col - 1)]

    for k in BACK_ORDER:
        width = PARTS[k][1]
        sent_l, sent_r = sent(k)
        pltpu.make_async_copy(sent_l, sent_l, out_sem.at[0, k]).wait()
        pltpu.make_async_copy(sent_r, sent_r, out_sem.at[1, k]).wait()

        def left_term(q, carry):
            right = recv_r[k][table[SS, q]]
            term = jnp.dot(weight[q], right, preferred_element_type=jnp.float32)
            before = mat[jnp.maximum(q - 1, 0), :, :width]
            mat[q, :, :width] = term + jnp.where(table[KF, q] > 0, before, 0.0)
            return carry

        lax.fori_loop(0, pairs, left_term, 0, unroll=UNROLL)

        def left_out(e, carry):
            for s in range(I_CAP):
                sums = mat[table[LF, e * I_CAP + s], :, :width]
                send_l[k][e * I_CAP + s] = sums.astype(jnp.bfloat16)

            @pl.when(e > 0)
            def _():
                for h in range(pieces):
                    back_l(k, h, e).start()

            return carry

        lax.fori_loop(0, n_row, left_out, 0)

        def right_term(t, carry):
            q = table[OS, t]
            left = recv_l[k][table[FS, q]]
            term = jnp.dot(weight_t[q], left, preferred_element_type=jnp.float32)
            before = mat[jnp.maximum(t - 1, 0), :, :width]
            mat[t, :, :width] = term + jnp.where(table[KS, t] > 0, before, 0.0)
            return carry

        lax.fori_loop(0, pairs, right_term, 0, unroll=UNROLL)

        def right_out(e, carry):
            send_r[k][e] = mat[table[LS, e], :, :width].astype(jnp.bfloat16)

            @pl.when(e > 0)
            def _():
                for h in range(pieces):
                    back_r(k, h, e).start()

            return carry

        lax.fori_loop(0, n_col, right_out, 0)
        for copy in own_copies(k):
            copy.start()

    def returned(k):
        for copy in own_copies(k):
            copy.wait()
        got_l = back[k].at[pl.ds(I_CAP, slots_f - I_CAP)]
        got_r = back[k].at[pl.ds(slots_f + 1, n_col - 1)]
        pltpu.make_async_copy(got_l, got_l, in_sem.at[2, k]).wait()
        pltpu.make_async_copy(got_r, got_r, in_sem.at[3, k]).wait()

    def store(n, k):
        start, width = PARTS[k]
        return pltpu.make_async_copy(
            mat.at[pl.ds(n % 2 * orb_dev, orb_dev), :, pl.ds(0, width)],
            part_sum.at[:, :, pl.ds(start, width)],
            sum_sem.at[1, n],
        )

    for n, k in enumerate(BACK_ORDER[:-1]):
        width = PARTS[k][1]
        stage = weight.at[:, :, pl.ds(0, width)]
        returned(k)
        fetch = pltpu.make_async_copy(back[k], stage, sum_sem.at[0, n])
        fetch.start()
        if n >= 2:
            store(n - 2, BACK_ORDER[n - 2]).wait()
        fetch.wait()

        def add_up(t, carry):
            rows = pl.ds(pl.multiple_of(t * SUM_ROWS, SUM_ROWS), SUM_ROWS)
            for o in range(orb_dev):
                total = jnp.zeros((SUM_ROWS, width), jnp.float32)
                for i in range(n_row + n_col):
                    at = pick[o, i]
                    term = weight[jnp.maximum(at, 0), rows, :width].astype(jnp.float32)
                    total = total + jnp.where(at >= 0, term, 0.0)
                mat[n % 2 * orb_dev + o, rows, :width] = total
            return carry

        lax.fori_loop(0, virtuals // SUM_ROWS, add_up, 0)
        store(n, k).start()

    returned(BACK_ORDER[-1])
    for n in range(max(parts - 3, 0), parts - 1):
        store(n, BACK_ORDER[n]).wait()
    for k in BACK_ORDER:
        sent_l, sent_r = sent(k)
        pltpu.make_async_copy(sent_l, sent_l, out_sem.at[2, k]).wait()
        pltpu.make_async_copy(sent_r, sent_r, out_sem.at[3, k]).wait()


def sum_kernel(n_row, n_col, asked, part_sum, back, out, listed, counts):
    orb_dev = out.shape[0]
    slots_f = n_row * I_CAP
    start, width = PARTS[BACK_ORDER[-1]]

    @pl.when(pl.program_id(0) == 0)
    def _():
        for o in range(8):
            counts[o] = 0

        def add(o, slot):
            at = counts[o]
            listed[o * 32 + at] = slot
            counts[o] = at + 1

        def firsts(e, carry):
            code = asked[e, e]
            add(code & 7, e * I_CAP)
            add(code >> 3, e * I_CAP + 1)
            return carry

        lax.fori_loop(0, n_row, firsts, 0)

        def seconds(e, carry):
            add(asked[n_row + e, n_row + e], slots_f + e)
            return carry

        lax.fori_loop(0, n_col, seconds, 0)

    for o in range(orb_dev):

        def add_slot(i, total):
            return total + back[listed[o * 32 + i]].astype(jnp.float32)

        zero = jnp.zeros(back.shape[1:], jnp.float32)
        out[o, :, start : start + width] = lax.fori_loop(0, counts[o], add_slot, zero)
    out[:, :, :start] = part_sum[...]


def shards(orbital_blocks, orbital_slot, pair_first, pair_second, occupied_energy, virtual_energy):
    n_row = lax.axis_size("row")
    n_col = lax.axis_size("col")
    orb_dev, virtuals, fitting = orbital_blocks.shape
    pairs = pair_first.shape[0]
    parts = len(PARTS)
    slots_f = n_row * I_CAP
    slots = slots_f + n_col
    summed = PARTS[BACK_ORDER[-1]][0]
    smem = pl.BlockSpec(memory_space=pltpu.SMEM)
    vmem = pl.BlockSpec(memory_space=pltpu.VMEM)
    hbm = pl.BlockSpec(memory_space=pl.ANY)

    def buffers(count):
        return [pltpu.VMEM((count, virtuals, width), jnp.bfloat16) for _, width in PARTS]

    *back, part_sum, asked = pl.pallas_call(
        functools.partial(pair_kernel, n_row, n_col),
        out_shape=(
            *[jax.ShapeDtypeStruct((slots, virtuals, width), jnp.bfloat16) for _, width in PARTS],
            jax.ShapeDtypeStruct((orb_dev, virtuals, summed), jnp.float32),
            jax.ShapeDtypeStruct((n_row + n_col, 128), jnp.int32),
        ),
        in_specs=[smem, smem, smem, smem, vmem, hbm],
        out_specs=(hbm,) * (parts + 1) + (smem,),
        scratch_shapes=[
            pltpu.VMEM((orb_dev, virtuals, fitting), jnp.bfloat16),
            buffers(slots_f),
            buffers(n_col),
            buffers(slots_f),
            buffers(n_col),
            pltpu.VMEM((pairs, virtuals, virtuals), jnp.float32),
            pltpu.VMEM((pairs, virtuals, virtuals), jnp.bfloat16),
            pltpu.VMEM((pairs, virtuals, virtuals), jnp.bfloat16),
            pltpu.VMEM((8, 128), jnp.int32),
            pltpu.VMEM((8, 128), jnp.float32),
            pltpu.SMEM((8, 128), jnp.int32),
            pltpu.SMEM((8, 128), jnp.float32),
            pltpu.SMEM((8, 32), jnp.int32),
            pltpu.SemaphoreType.DMA((3,)),
            pltpu.SemaphoreType.DMA((n_row + n_col,)),
            pltpu.SemaphoreType.DMA((n_row + n_col,)),
            pltpu.SemaphoreType.DMA((4, parts)),
            pltpu.SemaphoreType.DMA((4, parts)),
            pltpu.SemaphoreType.DMA((2, parts)),
            pltpu.SemaphoreType.DMA((2, parts)),
        ],
        compiler_params=pltpu.CompilerParams(
            collective_id=0, has_side_effects=True, vmem_limit_bytes=60 * 2**20
        ),
    )(
        orbital_slot,
        pair_first,
        pair_second,
        occupied_energy,
        virtual_energy.reshape(1, virtuals),
        orbital_blocks,
    )

    rows = 32
    width = PARTS[BACK_ORDER[-1]][1]
    return pl.pallas_call(
        functools.partial(sum_kernel, n_row, n_col),
        grid=(virtuals // rows,),
        out_shape=jax.ShapeDtypeStruct(orbital_blocks.shape, jnp.float32),
        in_specs=[
            smem,
            pl.BlockSpec((orb_dev, rows, summed), lambda i: (0, i, 0)),
            pl.BlockSpec((slots, rows, width), lambda i: (0, i, 0)),
        ],
        out_specs=pl.BlockSpec((orb_dev, rows, fitting), lambda i: (0, i, 0)),
        scratch_shapes=[pltpu.SMEM((8 * 32,), jnp.int32), pltpu.SMEM((8,), jnp.int32)],
        compiler_params=pltpu.CompilerParams(vmem_limit_bytes=60 * 2**20),
    )(asked, part_sum, back[BACK_ORDER[-1]])


def solution(mesh):
    return jax.shard_map(
        shards,
        mesh=mesh,
        in_specs=(
            P(("row", "col"), None, None),
            P(),
            P(("row", "col")),
            P(("row", "col")),
            P(),
            P(),
        ),
        out_specs=P(("row", "col"), None, None),
        check_vma=False,
    )
```

```python
import functools

import jax
import jax.numpy as jnp
from jax import lax
from jax.experimental import pallas as pl
from jax.experimental.pallas import tpu as pltpu
from jax.sharding import PartitionSpec as P

MESH = pl.DeviceIdType.MESH
I_CAP = 2
PARTS = ((0, 256), (256, 256), (512, 256), (768, 128), (896, 128))
BACK_ORDER = (3, 0, 1, 2, 4)
PIECE = 128
NONE = 7
FAR = 1 << 20
UNROLL = 16
SUM_ROWS = 16
ROWS = 128
ASK, FS, SS, KF, OS, KS, LF, LS = range(8)
ORDER, KEEP, LAST, SOME = range(4)


def row_step(row, e, sign):
    y = (row // 2 + sign * (e // 2) + 4) % 4
    k = (row % 2 + e % 2) % 2
    return y * 2 + k


def col_step(col, e, sign):
    z = (col // 4 + sign * (e // 4) + 4) % 4
    x = (col % 4 + sign * (e % 4) + 4) % 4
    return z * 4 + x


def plan(row, col, orb_dev, n_row, slot, first, second, occ, table, energy):
    pairs = first.shape[0]
    shape = (pairs, 128)
    lane = lax.broadcasted_iota(jnp.int32, shape, 1)
    sub = lax.broadcasted_iota(jnp.int32, shape, 0)
    shift = 16
    magic = (1 << shift) // orb_dev + 1

    def read(p, carry):
        f_down, f_across, s_down, s_across, e_down = carry
        i = first[p]
        j = second[p]
        pos_i = slot[i]
        pos_j = slot[j]
        dev_i = (pos_i * magic) >> shift
        dev_j = (pos_j * magic) >> shift
        row_i = dev_i >> 4
        col_j = dev_j & 15
        e_i = ((((row >> 1) - (row_i >> 1)) & 3) << 1) | ((row ^ row_i) & 1)
        e_j = ((((col >> 2) - (col_j >> 2)) & 3) << 2) | ((col - col_j) & 3)
        f = e_i * 8 + pos_i - dev_i * orb_dev
        s = e_j * 8 + pos_j - dev_j * orb_dev
        down = sub == p
        across = lane == p
        return (
            jnp.where(down, f, f_down),
            jnp.where(across, f, f_across),
            jnp.where(down, s, s_down),
            jnp.where(across, s, s_across),
            jnp.where(down, occ[i] + occ[j], e_down),
        )

    far = jnp.full(shape, FAR, jnp.int32)
    f_down, f_across, s_down, s_across, e_down = lax.fori_loop(
        0, pairs, read, (far, far, far, far, jnp.zeros(shape, jnp.float32)), unroll=8
    )

    def count(mask):
        return jnp.sum(mask.astype(jnp.int32), axis=1, keepdims=True)

    def line(values, keep):
        return jnp.sum(jnp.where(keep, values, jnp.zeros_like(values)), axis=0, keepdims=True)

    earlier = lane < sub
    same_f = f_across == f_down
    same_s = s_across == s_down
    rank_f = count((f_across < f_down) | (same_f & earlier))
    rank_s = count((s_across < s_down) | (same_s & earlier))
    behind = count(((f_across >> 3) == (f_down >> 3)) & (f_across < f_down)) > 0
    slot_f = (f_down >> 3) * I_CAP + behind.astype(jnp.int32)
    slot_s = s_down >> 3
    keep_f = (count(same_f & earlier) > 0).astype(jnp.int32) + jnp.zeros(shape, jnp.int32)
    keep_s = (count(same_s & earlier) > 0).astype(jnp.int32) + jnp.zeros(shape, jnp.int32)
    at_f = rank_f == lane
    at_s = rank_s == lane
    one = jnp.ones(shape, jnp.int32)
    mine_f = (f_down >> 3) == lane
    low = jnp.min(jnp.where(mine_f, f_down & 7, NONE), axis=0, keepdims=True)
    high = jnp.max(jnp.where(mine_f, f_down & 7, -1), axis=0, keepdims=True)
    ask_f = low + 8 * jnp.where(high > low, high, NONE)
    ask_s = jnp.min(jnp.where(slot_s == lane - n_row, s_down & 7, NONE), axis=0, keepdims=True)
    table[ASK : ASK + 1, :] = jnp.where(lane[:1] < n_row, ask_f, ask_s)
    table[FS : FS + 1, :] = line(slot_f, at_f)
    table[SS : SS + 1, :] = line(slot_s, at_f)
    table[KF : KF + 1, :] = line(keep_f, at_f)
    table[OS : OS + 1, :] = line(rank_f + jnp.zeros(shape, jnp.int32), at_s)
    table[KS : KS + 1, :] = line(keep_s, at_s)
    table[LF : LF + 1, :] = jnp.maximum(line(one, slot_f <= lane) - 1, 0)
    table[LS : LS + 1, :] = jnp.maximum(line(one, slot_s <= lane) - 1, 0)
    energy[0:1, :] = line(e_down, at_f)


def plan_owner(n_row, n_col, asked, owner):
    slots_f = n_row * I_CAP
    shape = (slots_f + n_col, 128)
    lane = lax.broadcasted_iota(jnp.int32, shape, 1)
    sub = lax.broadcasted_iota(jnp.int32, shape, 0)

    def put(at, local, carry):
        down, across = carry
        return jnp.where(sub == at, local, down), jnp.where(lane == at, local, across)

    def read_f(e, carry):
        code = asked[e, e]
        return put(e * I_CAP + 1, code >> 3, put(e * I_CAP, code & 7, carry))

    def read_s(e, carry):
        return put(slots_f + e, asked[n_row + e, n_row + e], carry)

    far = jnp.full(shape, FAR, jnp.int32)
    carry = lax.fori_loop(0, n_row, read_f, (far, far), unroll=4)
    down, across = lax.fori_loop(0, n_col, read_s, carry, unroll=4)
    before = (across == down) & (lane < sub)
    rank = jnp.sum(((across < down) | before).astype(jnp.int32), axis=1, keepdims=True)
    keep = jnp.minimum(jnp.sum(before.astype(jnp.int32), axis=1, keepdims=True), 1)
    here = rank == lane
    owner[ORDER : ORDER + 1, :] = jnp.sum(jnp.where(here, sub, 0), axis=0, keepdims=True)
    owner[KEEP : KEEP + 1, :] = jnp.sum(jnp.where(here, keep, 0), axis=0, keepdims=True)
    upto = jnp.sum((down <= lane).astype(jnp.int32), axis=0, keepdims=True)
    owner[LAST : LAST + 1, :] = jnp.maximum(upto - 1, 0)
    owner[SOME : SOME + 1, :] = jnp.max((down == lane).astype(jnp.int32), axis=0, keepdims=True)


def add_slots(owner, returned, runs, rows, width, orb_dev):
    total = jnp.zeros((runs.shape[1], width), jnp.float32)
    for t in range(runs.shape[0]):
        term = returned[owner[ORDER, t], rows, :width].astype(jnp.float32)
        total = term + jnp.where(owner[KEEP, t] > 0, total, 0.0)
        runs[t, :, :width] = total
    return [
        jnp.where(owner[SOME, o] > 0, runs[owner[LAST, o], :, :width], 0.0) for o in range(orb_dev)
    ]


def pair_kernel(
    n_row,
    n_col,
    slot,
    first,
    second,
    occ,
    energy_row,
    blocks_in,
    *refs,
):
    parts = len(PARTS)
    back = refs[:parts]
    part_sum, owner = refs[parts : parts + 2]
    (
        blocks,
        send_l,
        send_r,
        recv_l,
        recv_r,
        mat,
        weight,
        weight_t,
        table_v,
        energy_v,
        table,
        energy,
        asked,
        owner_v,
        runs,
        load_sem,
        ask_send,
        ask_recv,
        out_sem,
        in_sem,
        own_sem,
        sum_sem,
    ) = refs[parts + 2 :]
    row = lax.axis_index("row")
    col = lax.axis_index("col")
    orb_dev, virtuals, fitting = blocks.shape
    pairs = mat.shape[0]
    slots_f = n_row * I_CAP

    def to_row(e):
        return (row_step(row, e, 1), col)

    def to_col(e):
        return (row, col_step(col, e, 1))

    def from_row(e):
        return (row_step(row, e, -1), col)

    def from_col(e):
        return (row, col_step(col, e, -1))

    barrier = pltpu.get_barrier_semaphore()

    def greet(e, carry):
        pl.semaphore_signal(barrier, inc=1, device_id=to_col(e), device_id_type=MESH)

        @pl.when(e < n_row)
        def _():
            pl.semaphore_signal(barrier, inc=1, device_id=to_row(e), device_id_type=MESH)

        return carry

    lax.fori_loop(1, n_col, greet, 0)
    load = pltpu.make_async_copy(blocks_in, blocks, load_sem.at[0])
    load.start()
    plan(row, col, orb_dev, n_row, slot, first, second, occ, table_v, energy_v)
    to_scalar = (
        pltpu.make_async_copy(table_v, table, load_sem.at[1]),
        pltpu.make_async_copy(energy_v, energy, load_sem.at[2]),
    )
    for copy in to_scalar:
        copy.start()
    for copy in to_scalar:
        copy.wait()
    pl.semaphore_wait(barrier, n_row + n_col - 2)

    def ask_copy(place, target):
        return pltpu.make_async_remote_copy(
            src_ref=table.at[ASK],
            dst_ref=asked.at[place],
            send_sem=ask_send.at[place],
            recv_sem=ask_recv.at[place],
            device_id=target,
            device_id_type=MESH,
        )

    def ask(e, carry):
        ask_copy(n_row + e, from_col(e)).start()

        @pl.when(e < n_row)
        def _():
            ask_copy(e, from_row(e)).start()

        return carry

    lax.fori_loop(1, n_col, ask, 0)
    asked[0, 0] = table[ASK, 0]
    asked[n_row, n_row] = table[ASK, n_row]
    load.wait()

    def local_of(code):
        return jnp.where(code == NONE, 0, code)

    def copy_l(k, h, e):
        rows = pl.ds(h * PIECE, PIECE)
        place = pl.ds(e * I_CAP, I_CAP)
        return pltpu.make_async_remote_copy(
            src_ref=send_l[k].at[place, rows],
            dst_ref=recv_l[k].at[place, rows],
            send_sem=out_sem.at[0, k],
            recv_sem=in_sem.at[0, k],
            device_id=to_row(e),
            device_id_type=MESH,
        )

    def copy_r(k, h, e):
        rows = pl.ds(h * PIECE, PIECE)
        return pltpu.make_async_remote_copy(
            src_ref=send_r[k].at[e, rows],
            dst_ref=recv_r[k].at[e, rows],
            send_sem=out_sem.at[1, k],
            recv_sem=in_sem.at[1, k],
            device_id=to_col(e),
            device_id_type=MESH,
        )

    pieces = virtuals // PIECE
    for k, (start, width) in enumerate(PARTS):
        columns = slice(start, start + width)

        def forward(e, carry):
            if k == 0:
                ask_copy(n_row + e, from_col(e)).wait()
            send_r[k][e] = blocks[local_of(asked[n_row + e, n_row + e]), :, columns]
            copy_r(k, 0, e).start()

            @pl.when(e < n_row)
            def _():
                if k == 0:
                    ask_copy(e, from_row(e)).wait()
                code = asked[e, e]
                send_l[k][e * I_CAP] = blocks[local_of(code & 7), :, columns]
                send_l[k][e * I_CAP + 1] = blocks[local_of(code >> 3), :, columns]
                copy_l(k, 0, e).start()

            return carry

        lax.fori_loop(1, n_col, forward, 0)

        def forward_rest(e, carry):
            for h in range(1, pieces):
                copy_r(k, h, e).start()

                @pl.when(e < n_row)
                def _():
                    copy_l(k, h, e).start()

            return carry

        lax.fori_loop(1, n_col, forward_rest, 0)
        own = asked[0, 0]
        recv_l[k][0] = blocks[local_of(own & 7), :, columns]
        recv_l[k][1] = blocks[local_of(own >> 3), :, columns]
        recv_r[k][0] = blocks[local_of(asked[n_row, n_row]), :, columns]

    plan_owner(n_row, n_col, asked, owner_v)
    to_owner = pltpu.make_async_copy(owner_v, owner, load_sem.at[3])
    to_owner.start()

    virtual_row = jnp.broadcast_to(energy_row[...], (virtuals, virtuals))
    virtual_sum = virtual_row.T + virtual_row
    for k in range(parts):
        got_l = recv_l[k].at[pl.ds(I_CAP, slots_f - I_CAP)]
        got_r = recv_r[k].at[pl.ds(1, n_col - 1)]
        pltpu.make_async_copy(got_l, got_l, in_sem.at[0, k]).wait()
        pltpu.make_async_copy(got_r, got_r, in_sem.at[1, k]).wait()

        def integral(q, carry):
            left = recv_l[k][table[FS, q]]
            right = recv_r[k][table[SS, q]]
            found = lax.dot_general(
                left, right, (((1,), (1,)), ((), ())), preferred_element_type=jnp.float32
            )
            if k > 0:
                found = mat[q] + found
            if k < parts - 1:
                mat[q] = found
                return carry
            turned = found.T
            scale = 1.0 / (virtual_sum - energy[0, q])
            weight[q] = ((2.0 * found - turned) * scale).astype(jnp.bfloat16)
            weight_t[q] = ((2.0 * turned - found) * scale).astype(jnp.bfloat16)
            return carry

        lax.fori_loop(0, pairs, integral, 0, unroll=UNROLL)

    def back_l(k, h, e):
        rows = pl.ds(h * PIECE, PIECE)
        place = pl.ds(e * I_CAP, I_CAP)
        return pltpu.make_async_remote_copy(
            src_ref=send_l[k].at[place, rows],
            dst_ref=back[k].at[place, rows],
            send_sem=out_sem.at[2, k],
            recv_sem=in_sem.at[2, k],
            device_id=from_row(e),
            device_id_type=MESH,
        )

    def back_r(k, h, e):
        rows = pl.ds(h * PIECE, PIECE)
        return pltpu.make_async_remote_copy(
            src_ref=send_r[k].at[e, rows],
            dst_ref=back[k].at[slots_f + e, rows],
            send_sem=out_sem.at[3, k],
            recv_sem=in_sem.at[3, k],
            device_id=from_col(e),
            device_id_type=MESH,
        )

    def own_copies(k):
        own = pl.ds(0, I_CAP)
        return (
            pltpu.make_async_copy(send_l[k].at[own], back[k].at[own], own_sem.at[0, k]),
            pltpu.make_async_copy(send_r[k].at[0], back[k].at[slots_f], own_sem.at[1, k]),
        )

    def sent(k):
        return send_l[k].at[pl.ds(I_CAP, slots_f - I_CAP)], send_r[k].at[pl.ds(1, n_col - 1)]

    for k in BACK_ORDER:
        width = PARTS[k][1]
        sent_l, sent_r = sent(k)
        pltpu.make_async_copy(sent_l, sent_l, out_sem.at[0, k]).wait()
        pltpu.make_async_copy(sent_r, sent_r, out_sem.at[1, k]).wait()

        def run(terms, table_row, n):
            before = mat[jnp.maximum(n * UNROLL - 1, 0), :, :width]
            for u, term in enumerate(terms):
                before = term + jnp.where(table[table_row, n * UNROLL + u] > 0, before, 0.0)
                mat[n * UNROLL + u, :, :width] = before

        def left_terms(n, carry):
            terms = []
            for u in range(UNROLL):
                right = recv_r[k][table[SS, n * UNROLL + u]]
                terms.append(jnp.dot(weight[n * UNROLL + u], right, preferred_element_type=jnp.float32))
            run(terms, KF, n)
            return carry

        lax.fori_loop(0, pairs // UNROLL, left_terms, 0)

        def left_out(e, carry):
            for s in range(I_CAP):
                sums = mat[table[LF, e * I_CAP + s], :, :width]
                send_l[k][e * I_CAP + s] = sums.astype(jnp.bfloat16)
            return carry

        lax.fori_loop(0, n_row, left_out, 0)

        def right_terms(n, carry):
            terms = []
            for u in range(UNROLL):
                q = table[OS, n * UNROLL + u]
                left = recv_l[k][table[FS, q]]
                terms.append(jnp.dot(weight_t[q], left, preferred_element_type=jnp.float32))
            run(terms, KS, n)
            return carry

        lax.fori_loop(0, pairs // UNROLL, right_terms, 0)

        def right_out(e, carry):
            send_r[k][e] = mat[table[LS, e], :, :width].astype(jnp.bfloat16)
            back_r(k, 0, e).start()

            @pl.when(e < n_row)
            def _():
                back_l(k, 0, e).start()

            return carry

        lax.fori_loop(1, n_col, right_out, 0)

        def out_rest(e, carry):
            for h in range(1, pieces):
                back_r(k, h, e).start()

                @pl.when(e < n_row)
                def _():
                    back_l(k, h, e).start()

            return carry

        lax.fori_loop(1, n_col, out_rest, 0)
        send_r[k][0] = mat[table[LS, 0], :, :width].astype(jnp.bfloat16)
        for copy in own_copies(k):
            copy.start()

    def returned(k):
        for copy in own_copies(k):
            copy.wait()
        got_l = back[k].at[pl.ds(I_CAP, slots_f - I_CAP)]
        got_r = back[k].at[pl.ds(slots_f + 1, n_col - 1)]
        pltpu.make_async_copy(got_l, got_l, in_sem.at[2, k]).wait()
        pltpu.make_async_copy(got_r, got_r, in_sem.at[3, k]).wait()

    def store(n, k):
        start, width = PARTS[k]
        return pltpu.make_async_copy(
            mat.at[pl.ds(n % 2 * orb_dev, orb_dev), :, pl.ds(0, width)],
            part_sum.at[:, :, pl.ds(start, width)],
            sum_sem.at[1, n],
        )

    to_owner.wait()
    for n, k in enumerate(BACK_ORDER[:-1]):
        width = PARTS[k][1]
        stage = weight.at[:, :, pl.ds(0, width)]
        returned(k)
        fetch = pltpu.make_async_copy(back[k], stage, sum_sem.at[0, n])
        fetch.start()
        if n >= 2:
            store(n - 2, BACK_ORDER[n - 2]).wait()
        fetch.wait()

        def add_up(t, carry):
            rows = pl.ds(pl.multiple_of(t * SUM_ROWS, SUM_ROWS), SUM_ROWS)
            for o, total in enumerate(add_slots(owner, weight, runs, rows, width, orb_dev)):
                mat[n % 2 * orb_dev + o, rows, :width] = total
            return carry

        lax.fori_loop(0, virtuals // SUM_ROWS, add_up, 0)
        store(n, k).start()

    returned(BACK_ORDER[-1])
    for n in range(max(parts - 3, 0), parts - 1):
        store(n, BACK_ORDER[n]).wait()
    for k in BACK_ORDER:
        sent_l, sent_r = sent(k)
        pltpu.make_async_copy(sent_l, sent_l, out_sem.at[2, k]).wait()
        pltpu.make_async_copy(sent_r, sent_r, out_sem.at[3, k]).wait()


def sum_kernel(owner, part_sum, back, out, runs):
    orb_dev, rows, _ = out.shape
    start, width = PARTS[BACK_ORDER[-1]]
    for r in range(0, rows, SUM_ROWS):
        part = pl.ds(r, SUM_ROWS)
        for o, total in enumerate(add_slots(owner, back, runs, part, width, orb_dev)):
            out[o, part, start : start + width] = total
    out[:, :, :start] = part_sum[...]


def shards(orbital_blocks, orbital_slot, pair_first, pair_second, occupied_energy, virtual_energy):
    n_row = lax.axis_size("row")
    n_col = lax.axis_size("col")
    orb_dev, virtuals, fitting = orbital_blocks.shape
    pairs = pair_first.shape[0]
    parts = len(PARTS)
    slots_f = n_row * I_CAP
    slots = slots_f + n_col
    summed = PARTS[BACK_ORDER[-1]][0]
    smem = pl.BlockSpec(memory_space=pltpu.SMEM)
    vmem = pl.BlockSpec(memory_space=pltpu.VMEM)
    hbm = pl.BlockSpec(memory_space=pl.ANY)

    def buffers(count):
        return [pltpu.VMEM((count, virtuals, width), jnp.bfloat16) for _, width in PARTS]

    *back, part_sum, owner = pl.pallas_call(
        functools.partial(pair_kernel, n_row, n_col),
        out_shape=(
            *[jax.ShapeDtypeStruct((slots, virtuals, width), jnp.bfloat16) for _, width in PARTS],
            jax.ShapeDtypeStruct((orb_dev, virtuals, summed), jnp.float32),
            jax.ShapeDtypeStruct((8, 128), jnp.int32),
        ),
        in_specs=[smem, smem, smem, smem, vmem, hbm],
        out_specs=(hbm,) * (parts + 1) + (smem,),
        scratch_shapes=[
            pltpu.VMEM((orb_dev, virtuals, fitting), jnp.bfloat16),
            buffers(slots_f),
            buffers(n_col),
            buffers(slots_f),
            buffers(n_col),
            pltpu.VMEM((pairs, virtuals, virtuals), jnp.float32),
            pltpu.VMEM((pairs, virtuals, virtuals), jnp.bfloat16),
            pltpu.VMEM((pairs, virtuals, virtuals), jnp.bfloat16),
            pltpu.VMEM((8, 128), jnp.int32),
            pltpu.VMEM((8, 128), jnp.float32),
            pltpu.SMEM((8, 128), jnp.int32),
            pltpu.SMEM((8, 128), jnp.float32),
            pltpu.SMEM((n_row + n_col, 128), jnp.int32),
            pltpu.VMEM((8, 128), jnp.int32),
            pltpu.VMEM((slots, SUM_ROWS, 256), jnp.float32),
            pltpu.SemaphoreType.DMA((4,)),
            pltpu.SemaphoreType.DMA((n_row + n_col,)),
            pltpu.SemaphoreType.DMA((n_row + n_col,)),
            pltpu.SemaphoreType.DMA((4, parts)),
            pltpu.SemaphoreType.DMA((4, parts)),
            pltpu.SemaphoreType.DMA((2, parts)),
            pltpu.SemaphoreType.DMA((2, parts)),
        ],
        compiler_params=pltpu.CompilerParams(
            collective_id=0, has_side_effects=True, vmem_limit_bytes=60 * 2**20
        ),
    )(
        orbital_slot,
        pair_first,
        pair_second,
        occupied_energy,
        virtual_energy.reshape(1, virtuals),
        orbital_blocks,
    )

    rows = ROWS
    width = PARTS[BACK_ORDER[-1]][1]
    return pl.pallas_call(
        sum_kernel,
        grid=(virtuals // rows,),
        out_shape=jax.ShapeDtypeStruct(orbital_blocks.shape, jnp.float32),
        in_specs=[
            smem,
            pl.BlockSpec((orb_dev, rows, summed), lambda i: (0, i, 0)),
            pl.BlockSpec((slots, rows, width), lambda i: (0, i, 0)),
        ],
        out_specs=pl.BlockSpec((orb_dev, rows, fitting), lambda i: (0, i, 0)),
        scratch_shapes=[pltpu.VMEM((slots, SUM_ROWS, width), jnp.float32)],
        compiler_params=pltpu.CompilerParams(vmem_limit_bytes=60 * 2**20),
    )(owner, part_sum, back[BACK_ORDER[-1]])


def solution(mesh):
    return jax.shard_map(
        shards,
        mesh=mesh,
        in_specs=(
            P(("row", "col"), None, None),
            P(),
            P(("row", "col")),
            P(("row", "col")),
            P(),
            P(),
        ),
        out_specs=P(("row", "col"), None, None),
        check_vma=False,
    )
```

```python
import functools

import jax
import jax.numpy as jnp
from jax import lax
from jax.experimental import pallas as pl
from jax.experimental.pallas import tpu as pltpu
from jax.sharding import PartitionSpec as P

MESH = pl.DeviceIdType.MESH
I_CAP = 2
PARTS = ((0, 256), (256, 256), (512, 256), (768, 128), (896, 128))
BACK_ORDER = (3, 0, 1, 2, 4)
PIECE = 128
NONE = 7
FAR = 1 << 20
UNROLL = 16
SUM_ROWS = 16
ROWS = 128
ASK, FS, SS, KF, OS, KS, LF, LS = range(8)
ORDER, KEEP, LAST, SOME = range(4)


def row_step(row, e, sign):
    y = (row // 2 + sign * (e // 2) + 4) % 4
    k = (row % 2 + e % 2) % 2
    return y * 2 + k


def col_step(col, e, sign):
    z = (col // 4 + sign * (e // 4) + 4) % 4
    x = (col % 4 + sign * (e % 4) + 4) % 4
    return z * 4 + x


def plan(row, col, orb_dev, n_row, slot, first, second, occ, table, energy):
    pairs = first.shape[0]
    shape = (pairs, 128)
    lane = lax.broadcasted_iota(jnp.int32, shape, 1)
    sub = lax.broadcasted_iota(jnp.int32, shape, 0)
    shift = 16
    magic = (1 << shift) // orb_dev + 1

    def read(p, carry):
        f_down, f_across, s_down, s_across, e_down = carry
        i = first[p]
        j = second[p]
        pos_i = slot[i]
        pos_j = slot[j]
        dev_i = (pos_i * magic) >> shift
        dev_j = (pos_j * magic) >> shift
        row_i = dev_i >> 4
        col_j = dev_j & 15
        e_i = ((((row >> 1) - (row_i >> 1)) & 3) << 1) | ((row ^ row_i) & 1)
        e_j = ((((col >> 2) - (col_j >> 2)) & 3) << 2) | ((col - col_j) & 3)
        f = e_i * 8 + pos_i - dev_i * orb_dev
        s = e_j * 8 + pos_j - dev_j * orb_dev
        down = sub == p
        across = lane == p
        return (
            jnp.where(down, f, f_down),
            jnp.where(across, f, f_across),
            jnp.where(down, s, s_down),
            jnp.where(across, s, s_across),
            jnp.where(down, occ[i] + occ[j], e_down),
        )

    far = jnp.full(shape, FAR, jnp.int32)
    f_down, f_across, s_down, s_across, e_down = lax.fori_loop(
        0, pairs, read, (far, far, far, far, jnp.zeros(shape, jnp.float32)), unroll=8
    )

    def count(mask):
        return jnp.sum(mask.astype(jnp.int32), axis=1, keepdims=True)

    def line(values, keep):
        return jnp.sum(jnp.where(keep, values, jnp.zeros_like(values)), axis=0, keepdims=True)

    earlier = lane < sub
    same_f = f_across == f_down
    same_s = s_across == s_down
    rank_f = count((f_across < f_down) | (same_f & earlier))
    rank_s = count((s_across < s_down) | (same_s & earlier))
    behind = count(((f_across >> 3) == (f_down >> 3)) & (f_across < f_down)) > 0
    slot_f = (f_down >> 3) * I_CAP + behind.astype(jnp.int32)
    slot_s = s_down >> 3
    keep_f = (count(same_f & earlier) > 0).astype(jnp.int32) + jnp.zeros(shape, jnp.int32)
    keep_s = (count(same_s & earlier) > 0).astype(jnp.int32) + jnp.zeros(shape, jnp.int32)
    at_f = rank_f == lane
    at_s = rank_s == lane
    one = jnp.ones(shape, jnp.int32)
    mine_f = (f_down >> 3) == lane
    low = jnp.min(jnp.where(mine_f, f_down & 7, NONE), axis=0, keepdims=True)
    high = jnp.max(jnp.where(mine_f, f_down & 7, -1), axis=0, keepdims=True)
    ask_f = low + 8 * jnp.where(high > low, high, NONE)
    ask_s = jnp.min(jnp.where(slot_s == lane - n_row, s_down & 7, NONE), axis=0, keepdims=True)
    table[ASK : ASK + 1, :] = jnp.where(lane[:1] < n_row, ask_f, ask_s)
    table[FS : FS + 1, :] = line(slot_f, at_f)
    table[SS : SS + 1, :] = line(slot_s, at_f)
    table[KF : KF + 1, :] = line(keep_f, at_f)
    table[OS : OS + 1, :] = line(rank_f + jnp.zeros(shape, jnp.int32), at_s)
    table[KS : KS + 1, :] = line(keep_s, at_s)
    table[LF : LF + 1, :] = jnp.maximum(line(one, slot_f <= lane) - 1, 0)
    table[LS : LS + 1, :] = jnp.maximum(line(one, slot_s <= lane) - 1, 0)
    energy[0:1, :] = line(e_down, at_f)


def plan_owner(n_row, n_col, asked, owner):
    slots_f = n_row * I_CAP
    shape = (slots_f + n_col, 128)
    lane = lax.broadcasted_iota(jnp.int32, shape, 1)
    sub = lax.broadcasted_iota(jnp.int32, shape, 0)

    def put(at, local, carry):
        down, across = carry
        return jnp.where(sub == at, local, down), jnp.where(lane == at, local, across)

    def read_f(e, carry):
        code = asked[e, e]
        return put(e * I_CAP + 1, code >> 3, put(e * I_CAP, code & 7, carry))

    def read_s(e, carry):
        return put(slots_f + e, asked[n_row + e, n_row + e], carry)

    far = jnp.full(shape, FAR, jnp.int32)
    carry = lax.fori_loop(0, n_row, read_f, (far, far), unroll=4)
    down, across = lax.fori_loop(0, n_col, read_s, carry, unroll=4)
    before = (across == down) & (lane < sub)
    rank = jnp.sum(((across < down) | before).astype(jnp.int32), axis=1, keepdims=True)
    keep = jnp.minimum(jnp.sum(before.astype(jnp.int32), axis=1, keepdims=True), 1)
    here = rank == lane
    owner[ORDER : ORDER + 1, :] = jnp.sum(jnp.where(here, sub, 0), axis=0, keepdims=True)
    owner[KEEP : KEEP + 1, :] = jnp.sum(jnp.where(here, keep, 0), axis=0, keepdims=True)
    upto = jnp.sum((down <= lane).astype(jnp.int32), axis=0, keepdims=True)
    owner[LAST : LAST + 1, :] = jnp.maximum(upto - 1, 0)
    owner[SOME : SOME + 1, :] = jnp.max((down == lane).astype(jnp.int32), axis=0, keepdims=True)


def add_slots(owner, returned, runs, rows, width, orb_dev):
    total = jnp.zeros((runs.shape[1], width), jnp.float32)
    for t in range(runs.shape[0]):
        term = returned[owner[ORDER, t], rows, :width].astype(jnp.float32)
        total = term + jnp.where(owner[KEEP, t] > 0, total, 0.0)
        runs[t, :, :width] = total
    return [
        jnp.where(owner[SOME, o] > 0, runs[owner[LAST, o], :, :width], 0.0) for o in range(orb_dev)
    ]


def pair_kernel(
    n_row,
    n_col,
    slot,
    first,
    second,
    occ,
    energy_row,
    blocks_in,
    *refs,
):
    parts = len(PARTS)
    back = refs[:parts]
    part_sum, owner = refs[parts : parts + 2]
    (
        blocks,
        send_l,
        send_r,
        recv_l,
        recv_r,
        mat,
        weight,
        weight_t,
        table_v,
        energy_v,
        table,
        energy,
        asked,
        owner_v,
        runs,
        load_sem,
        ask_send,
        ask_recv,
        out_sem,
        in_sem,
        own_sem,
        sum_sem,
    ) = refs[parts + 2 :]
    row = lax.axis_index("row")
    col = lax.axis_index("col")
    orb_dev, virtuals, fitting = blocks.shape
    pairs = mat.shape[0]
    slots_f = n_row * I_CAP

    def to_row(e):
        return (row_step(row, e, 1), col)

    def to_col(e):
        return (row, col_step(col, e, 1))

    def from_row(e):
        return (row_step(row, e, -1), col)

    def from_col(e):
        return (row, col_step(col, e, -1))

    barrier = pltpu.get_barrier_semaphore()

    def greet(e, carry):
        pl.semaphore_signal(barrier, inc=1, device_id=to_col(e), device_id_type=MESH)

        @pl.when(e < n_row)
        def _():
            pl.semaphore_signal(barrier, inc=1, device_id=to_row(e), device_id_type=MESH)

        return carry

    lax.fori_loop(1, n_col, greet, 0)
    load = pltpu.make_async_copy(blocks_in, blocks, load_sem.at[0])
    load.start()
    plan(row, col, orb_dev, n_row, slot, first, second, occ, table_v, energy_v)
    to_scalar = (
        pltpu.make_async_copy(table_v, table, load_sem.at[1]),
        pltpu.make_async_copy(energy_v, energy, load_sem.at[2]),
    )
    for copy in to_scalar:
        copy.start()
    for copy in to_scalar:
        copy.wait()
    pl.semaphore_wait(barrier, n_row + n_col - 2)

    def ask_copy(place, target):
        return pltpu.make_async_remote_copy(
            src_ref=table.at[ASK],
            dst_ref=asked.at[place],
            send_sem=ask_send.at[place],
            recv_sem=ask_recv.at[place],
            device_id=target,
            device_id_type=MESH,
        )

    def ask(e, carry):
        ask_copy(n_row + e, from_col(e)).start()

        @pl.when(e < n_row)
        def _():
            ask_copy(e, from_row(e)).start()

        return carry

    lax.fori_loop(1, n_col, ask, 0)
    asked[0, 0] = table[ASK, 0]
    asked[n_row, n_row] = table[ASK, n_row]
    load.wait()

    def local_of(code):
        return jnp.where(code == NONE, 0, code)

    def copy_l(k, h, e):
        rows = pl.ds(h * PIECE, PIECE)
        place = pl.ds(e * I_CAP, I_CAP)
        return pltpu.make_async_remote_copy(
            src_ref=send_l[k].at[place, rows],
            dst_ref=recv_l[k].at[place, rows],
            send_sem=out_sem.at[0, k],
            recv_sem=in_sem.at[0, k],
            device_id=to_row(e),
            device_id_type=MESH,
        )

    def copy_r(k, h, e):
        rows = pl.ds(h * PIECE, PIECE)
        return pltpu.make_async_remote_copy(
            src_ref=send_r[k].at[e, rows],
            dst_ref=recv_r[k].at[e, rows],
            send_sem=out_sem.at[1, k],
            recv_sem=in_sem.at[1, k],
            device_id=to_col(e),
            device_id_type=MESH,
        )

    pieces = virtuals // PIECE
    for k, (start, width) in enumerate(PARTS):
        columns = slice(start, start + width)

        def forward(e, carry):
            if k == 0:
                ask_copy(n_row + e, from_col(e)).wait()
            send_r[k][e] = blocks[local_of(asked[n_row + e, n_row + e]), :, columns]
            copy_r(k, 0, e).start()

            @pl.when(e < n_row)
            def _():
                if k == 0:
                    ask_copy(e, from_row(e)).wait()
                code = asked[e, e]
                send_l[k][e * I_CAP] = blocks[local_of(code & 7), :, columns]
                send_l[k][e * I_CAP + 1] = blocks[local_of(code >> 3), :, columns]
                copy_l(k, 0, e).start()

            return carry

        lax.fori_loop(1, n_col, forward, 0)

        def forward_rest(e, carry):
            for h in range(1, pieces):
                copy_r(k, h, e).start()

                @pl.when(e < n_row)
                def _():
                    copy_l(k, h, e).start()

            return carry

        lax.fori_loop(1, n_col, forward_rest, 0)
        own = asked[0, 0]
        recv_l[k][0] = blocks[local_of(own & 7), :, columns]
        recv_l[k][1] = blocks[local_of(own >> 3), :, columns]
        recv_r[k][0] = blocks[local_of(asked[n_row, n_row]), :, columns]

    plan_owner(n_row, n_col, asked, owner_v)
    to_owner = pltpu.make_async_copy(owner_v, owner, load_sem.at[3])
    to_owner.start()

    virtual_row = jnp.broadcast_to(energy_row[...], (virtuals, virtuals))
    virtual_sum = virtual_row.T + virtual_row
    for k in range(parts):
        got_l = recv_l[k].at[pl.ds(I_CAP, slots_f - I_CAP)]
        got_r = recv_r[k].at[pl.ds(1, n_col - 1)]
        pltpu.make_async_copy(got_l, got_l, in_sem.at[0, k]).wait()
        pltpu.make_async_copy(got_r, got_r, in_sem.at[1, k]).wait()

        def integral(q, carry):
            left = recv_l[k][table[FS, q]]
            right = recv_r[k][table[SS, q]]
            found = lax.dot_general(
                left, right, (((1,), (1,)), ((), ())), preferred_element_type=jnp.float32
            )
            if k > 0:
                found = mat[q] + found
            if k < parts - 1:
                mat[q] = found
                return carry
            turned = found.T
            scale = 1.0 / (virtual_sum - energy[0, q])
            weight[q] = ((2.0 * found - turned) * scale).astype(jnp.bfloat16)
            weight_t[q] = ((2.0 * turned - found) * scale).astype(jnp.bfloat16)
            return carry

        lax.fori_loop(0, pairs, integral, 0, unroll=UNROLL)

    def back_l(k, h, e):
        rows = pl.ds(h * PIECE, PIECE)
        place = pl.ds(e * I_CAP, I_CAP)
        return pltpu.make_async_remote_copy(
            src_ref=send_l[k].at[place, rows],
            dst_ref=back[k].at[place, rows],
            send_sem=out_sem.at[2, k],
            recv_sem=in_sem.at[2, k],
            device_id=from_row(e),
            device_id_type=MESH,
        )

    def back_r(k, h, e):
        rows = pl.ds(h * PIECE, PIECE)
        return pltpu.make_async_remote_copy(
            src_ref=send_r[k].at[e, rows],
            dst_ref=back[k].at[slots_f + e, rows],
            send_sem=out_sem.at[3, k],
            recv_sem=in_sem.at[3, k],
            device_id=from_col(e),
            device_id_type=MESH,
        )

    def own_copies(k):
        own = pl.ds(0, I_CAP)
        return (
            pltpu.make_async_copy(send_l[k].at[own], back[k].at[own], own_sem.at[0, k]),
            pltpu.make_async_copy(send_r[k].at[0], back[k].at[slots_f], own_sem.at[1, k]),
        )

    def sent(k):
        return send_l[k].at[pl.ds(I_CAP, slots_f - I_CAP)], send_r[k].at[pl.ds(1, n_col - 1)]

    for k in BACK_ORDER:
        width = PARTS[k][1]
        sent_l, sent_r = sent(k)
        pltpu.make_async_copy(sent_l, sent_l, out_sem.at[0, k]).wait()
        pltpu.make_async_copy(sent_r, sent_r, out_sem.at[1, k]).wait()

        def run(terms, table_row, n):
            before = mat[jnp.maximum(n * UNROLL - 1, 0), :, :width]
            for u, term in enumerate(terms):
                before = term + jnp.where(table[table_row, n * UNROLL + u] > 0, before, 0.0)
                mat[n * UNROLL + u, :, :width] = before

        def left_terms(n, carry):
            terms = []
            for u in range(UNROLL):
                right = recv_r[k][table[SS, n * UNROLL + u]]
                terms.append(jnp.dot(weight[n * UNROLL + u], right, preferred_element_type=jnp.float32))
            run(terms, KF, n)
            return carry

        def right_terms(n, carry):
            terms = []
            for u in range(UNROLL):
                q = table[OS, n * UNROLL + u]
                left = recv_l[k][table[FS, q]]
                terms.append(jnp.dot(weight_t[q], left, preferred_element_type=jnp.float32))
            run(terms, KS, n)
            return carry

        def left_out(e, carry):
            for s in range(I_CAP):
                sums = mat[table[LF, e * I_CAP + s], :, :width]
                send_l[k][e * I_CAP + s] = sums.astype(jnp.bfloat16)
            return carry

        def right_out(e, carry):
            send_r[k][e] = mat[table[LS, e], :, :width].astype(jnp.bfloat16)
            return carry

        def send_right(e, carry):
            for h in range(pieces):
                back_r(k, h, e).start()
            return carry

        def send_left(e, carry):
            for h in range(pieces):
                back_l(k, h, e).start()
            return carry

        def send_both(h):
            def send(e, carry):
                back_r(k, h, e).start()

                @pl.when(e < n_row)
                def _():
                    back_l(k, h, e).start()

                return carry

            return send

        lax.fori_loop(0, pairs // UNROLL, right_terms, 0)
        lax.fori_loop(0, n_col, right_out, 0)
        if k == BACK_ORDER[0]:
            lax.fori_loop(1, n_col, send_right, 0)
        lax.fori_loop(0, pairs // UNROLL, left_terms, 0)
        lax.fori_loop(0, n_row, left_out, 0)
        if k == BACK_ORDER[0]:
            lax.fori_loop(1, n_row, send_left, 0)
        else:
            for h in range(pieces):
                lax.fori_loop(1, n_col, send_both(h), 0)
        for copy in own_copies(k):
            copy.start()

    def returned(k):
        for copy in own_copies(k):
            copy.wait()
        got_l = back[k].at[pl.ds(I_CAP, slots_f - I_CAP)]
        got_r = back[k].at[pl.ds(slots_f + 1, n_col - 1)]
        pltpu.make_async_copy(got_l, got_l, in_sem.at[2, k]).wait()
        pltpu.make_async_copy(got_r, got_r, in_sem.at[3, k]).wait()

    def store(n, k):
        start, width = PARTS[k]
        return pltpu.make_async_copy(
            mat.at[pl.ds(n % 2 * orb_dev, orb_dev), :, pl.ds(0, width)],
            part_sum.at[:, :, pl.ds(start, width)],
            sum_sem.at[1, n],
        )

    to_owner.wait()
    for n, k in enumerate(BACK_ORDER[:-1]):
        width = PARTS[k][1]
        stage = weight.at[:, :, pl.ds(0, width)]
        returned(k)
        fetch = pltpu.make_async_copy(back[k], stage, sum_sem.at[0, n])
        fetch.start()
        if n >= 2:
            store(n - 2, BACK_ORDER[n - 2]).wait()
        fetch.wait()

        def add_up(t, carry):
            rows = pl.ds(pl.multiple_of(t * SUM_ROWS, SUM_ROWS), SUM_ROWS)
            for o, total in enumerate(add_slots(owner, weight, runs, rows, width, orb_dev)):
                mat[n % 2 * orb_dev + o, rows, :width] = total
            return carry

        lax.fori_loop(0, virtuals // SUM_ROWS, add_up, 0)
        store(n, k).start()

    returned(BACK_ORDER[-1])
    for n in range(max(parts - 3, 0), parts - 1):
        store(n, BACK_ORDER[n]).wait()
    for k in BACK_ORDER:
        sent_l, sent_r = sent(k)
        pltpu.make_async_copy(sent_l, sent_l, out_sem.at[2, k]).wait()
        pltpu.make_async_copy(sent_r, sent_r, out_sem.at[3, k]).wait()


def sum_kernel(owner, part_sum, back, out, runs):
    orb_dev, rows, _ = out.shape
    start, width = PARTS[BACK_ORDER[-1]]
    for r in range(0, rows, SUM_ROWS):
        part = pl.ds(r, SUM_ROWS)
        for o, total in enumerate(add_slots(owner, back, runs, part, width, orb_dev)):
            out[o, part, start : start + width] = total
    out[:, :, :start] = part_sum[...]


def shards(orbital_blocks, orbital_slot, pair_first, pair_second, occupied_energy, virtual_energy):
    n_row = lax.axis_size("row")
    n_col = lax.axis_size("col")
    orb_dev, virtuals, fitting = orbital_blocks.shape
    pairs = pair_first.shape[0]
    parts = len(PARTS)
    slots_f = n_row * I_CAP
    slots = slots_f + n_col
    summed = PARTS[BACK_ORDER[-1]][0]
    smem = pl.BlockSpec(memory_space=pltpu.SMEM)
    vmem = pl.BlockSpec(memory_space=pltpu.VMEM)
    hbm = pl.BlockSpec(memory_space=pl.ANY)

    def buffers(count):
        return [pltpu.VMEM((count, virtuals, width), jnp.bfloat16) for _, width in PARTS]

    *back, part_sum, owner = pl.pallas_call(
        functools.partial(pair_kernel, n_row, n_col),
        out_shape=(
            *[jax.ShapeDtypeStruct((slots, virtuals, width), jnp.bfloat16) for _, width in PARTS],
            jax.ShapeDtypeStruct((orb_dev, virtuals, summed), jnp.float32),
            jax.ShapeDtypeStruct((8, 128), jnp.int32),
        ),
        in_specs=[smem, smem, smem, smem, vmem, hbm],
        out_specs=(hbm,) * (parts + 1) + (smem,),
        scratch_shapes=[
            pltpu.VMEM((orb_dev, virtuals, fitting), jnp.bfloat16),
            buffers(slots_f),
            buffers(n_col),
            buffers(slots_f),
            buffers(n_col),
            pltpu.VMEM((pairs, virtuals, virtuals), jnp.float32),
            pltpu.VMEM((pairs, virtuals, virtuals), jnp.bfloat16),
            pltpu.VMEM((pairs, virtuals, virtuals), jnp.bfloat16),
            pltpu.VMEM((8, 128), jnp.int32),
            pltpu.VMEM((8, 128), jnp.float32),
            pltpu.SMEM((8, 128), jnp.int32),
            pltpu.SMEM((8, 128), jnp.float32),
            pltpu.SMEM((n_row + n_col, 128), jnp.int32),
            pltpu.VMEM((8, 128), jnp.int32),
            pltpu.VMEM((slots, SUM_ROWS, 256), jnp.float32),
            pltpu.SemaphoreType.DMA((4,)),
            pltpu.SemaphoreType.DMA((n_row + n_col,)),
            pltpu.SemaphoreType.DMA((n_row + n_col,)),
            pltpu.SemaphoreType.DMA((4, parts)),
            pltpu.SemaphoreType.DMA((4, parts)),
            pltpu.SemaphoreType.DMA((2, parts)),
            pltpu.SemaphoreType.DMA((2, parts)),
        ],
        compiler_params=pltpu.CompilerParams(
            collective_id=0, has_side_effects=True, vmem_limit_bytes=60 * 2**20
        ),
    )(
        orbital_slot,
        pair_first,
        pair_second,
        occupied_energy,
        virtual_energy.reshape(1, virtuals),
        orbital_blocks,
    )

    rows = ROWS
    width = PARTS[BACK_ORDER[-1]][1]
    return pl.pallas_call(
        sum_kernel,
        grid=(virtuals // rows,),
        out_shape=jax.ShapeDtypeStruct(orbital_blocks.shape, jnp.float32),
        in_specs=[
            smem,
            pl.BlockSpec((orb_dev, rows, summed), lambda i: (0, i, 0)),
            pl.BlockSpec((slots, rows, width), lambda i: (0, i, 0)),
        ],
        out_specs=pl.BlockSpec((orb_dev, rows, fitting), lambda i: (0, i, 0)),
        scratch_shapes=[pltpu.VMEM((slots, SUM_ROWS, width), jnp.float32)],
        compiler_params=pltpu.CompilerParams(vmem_limit_bytes=60 * 2**20),
    )(owner, part_sum, back[BACK_ORDER[-1]])


def solution(mesh):
    return jax.shard_map(
        shards,
        mesh=mesh,
        in_specs=(
            P(("row", "col"), None, None),
            P(),
            P(("row", "col")),
            P(("row", "col")),
            P(),
            P(),
        ),
        out_specs=P(("row", "col"), None, None),
        check_vma=False,
    )
```

```python
import functools

import jax
import jax.numpy as jnp
from jax import lax
from jax.experimental import pallas as pl
from jax.experimental.pallas import tpu as pltpu
from jax.sharding import PartitionSpec as P

MESH = pl.DeviceIdType.MESH
I_CAP = 2
PARTS = ((0, 256), (256, 256), (512, 256), (768, 128), (896, 128))
BACK_ORDER = (3, 0, 1, 2, 4)
PIECE = 128
NONE = 7
FAR = 1 << 20
UNROLL = 16
SUM_ROWS = 16
ROWS = 128
ASK, FS, SS, KF, OS, KS, LF, LS = range(8)
ORDER, KEEP, LAST, SOME = range(4)


def row_step(row, e, sign):
    y = (row // 2 + sign * (e // 2) + 4) % 4
    k = (row % 2 + e % 2) % 2
    return y * 2 + k


def col_step(col, e, sign):
    z = (col // 4 + sign * (e // 4) + 4) % 4
    x = (col % 4 + sign * (e % 4) + 4) % 4
    return z * 4 + x


def plan(row, col, orb_dev, n_row, slot, first, second, occ, table, energy):
    pairs = first.shape[0]
    shape = (pairs, 128)
    lane = lax.broadcasted_iota(jnp.int32, shape, 1)
    sub = lax.broadcasted_iota(jnp.int32, shape, 0)
    shift = 16
    magic = (1 << shift) // orb_dev + 1

    def read(p, carry):
        f_down, f_across, s_down, s_across, e_down = carry
        i = first[p]
        j = second[p]
        pos_i = slot[i]
        pos_j = slot[j]
        dev_i = (pos_i * magic) >> shift
        dev_j = (pos_j * magic) >> shift
        row_i = dev_i >> 4
        col_j = dev_j & 15
        e_i = ((((row >> 1) - (row_i >> 1)) & 3) << 1) | ((row ^ row_i) & 1)
        e_j = ((((col >> 2) - (col_j >> 2)) & 3) << 2) | ((col - col_j) & 3)
        f = e_i * 8 + pos_i - dev_i * orb_dev
        s = e_j * 8 + pos_j - dev_j * orb_dev
        down = sub == p
        across = lane == p
        return (
            jnp.where(down, f, f_down),
            jnp.where(across, f, f_across),
            jnp.where(down, s, s_down),
            jnp.where(across, s, s_across),
            jnp.where(down, occ[i] + occ[j], e_down),
        )

    far = jnp.full(shape, FAR, jnp.int32)
    f_down, f_across, s_down, s_across, e_down = lax.fori_loop(
        0, pairs, read, (far, far, far, far, jnp.zeros(shape, jnp.float32)), unroll=8
    )

    def count(mask):
        return jnp.sum(mask.astype(jnp.int32), axis=1, keepdims=True)

    def line(values, keep):
        return jnp.sum(jnp.where(keep, values, jnp.zeros_like(values)), axis=0, keepdims=True)

    earlier = lane < sub
    same_f = f_across == f_down
    same_s = s_across == s_down
    rank_f = count((f_across < f_down) | (same_f & earlier))
    rank_s = count((s_across < s_down) | (same_s & earlier))
    behind = count(((f_across >> 3) == (f_down >> 3)) & (f_across < f_down)) > 0
    slot_f = (f_down >> 3) * I_CAP + behind.astype(jnp.int32)
    slot_s = s_down >> 3
    keep_f = (count(same_f & earlier) > 0).astype(jnp.int32) + jnp.zeros(shape, jnp.int32)
    keep_s = (count(same_s & earlier) > 0).astype(jnp.int32) + jnp.zeros(shape, jnp.int32)
    at_f = rank_f == lane
    at_s = rank_s == lane
    one = jnp.ones(shape, jnp.int32)
    mine_f = (f_down >> 3) == lane
    low = jnp.min(jnp.where(mine_f, f_down & 7, NONE), axis=0, keepdims=True)
    high = jnp.max(jnp.where(mine_f, f_down & 7, -1), axis=0, keepdims=True)
    ask_f = low + 8 * jnp.where(high > low, high, NONE)
    ask_s = jnp.min(jnp.where(slot_s == lane - n_row, s_down & 7, NONE), axis=0, keepdims=True)
    table[ASK : ASK + 1, :] = jnp.where(lane[:1] < n_row, ask_f, ask_s)
    table[FS : FS + 1, :] = line(slot_f, at_f)
    table[SS : SS + 1, :] = line(slot_s, at_f)
    table[KF : KF + 1, :] = line(keep_f, at_f)
    table[OS : OS + 1, :] = line(rank_f + jnp.zeros(shape, jnp.int32), at_s)
    table[KS : KS + 1, :] = line(keep_s, at_s)
    table[LF : LF + 1, :] = jnp.maximum(line(one, slot_f <= lane) - 1, 0)
    table[LS : LS + 1, :] = jnp.maximum(line(one, slot_s <= lane) - 1, 0)
    energy[0:1, :] = line(e_down, at_f)


def plan_owner(n_row, n_col, asked, owner):
    slots_f = n_row * I_CAP
    shape = (slots_f + n_col, 128)
    lane = lax.broadcasted_iota(jnp.int32, shape, 1)
    sub = lax.broadcasted_iota(jnp.int32, shape, 0)

    def put(at, local, carry):
        down, across = carry
        return jnp.where(sub == at, local, down), jnp.where(lane == at, local, across)

    def read_f(e, carry):
        code = asked[e, e]
        return put(e * I_CAP + 1, code >> 3, put(e * I_CAP, code & 7, carry))

    def read_s(e, carry):
        return put(slots_f + e, asked[n_row + e, n_row + e], carry)

    far = jnp.full(shape, FAR, jnp.int32)
    carry = lax.fori_loop(0, n_row, read_f, (far, far), unroll=4)
    down, across = lax.fori_loop(0, n_col, read_s, carry, unroll=4)
    before = (across == down) & (lane < sub)
    rank = jnp.sum(((across < down) | before).astype(jnp.int32), axis=1, keepdims=True)
    keep = jnp.minimum(jnp.sum(before.astype(jnp.int32), axis=1, keepdims=True), 1)
    here = rank == lane
    owner[ORDER : ORDER + 1, :] = jnp.sum(jnp.where(here, sub, 0), axis=0, keepdims=True)
    owner[KEEP : KEEP + 1, :] = jnp.sum(jnp.where(here, keep, 0), axis=0, keepdims=True)
    upto = jnp.sum((down <= lane).astype(jnp.int32), axis=0, keepdims=True)
    owner[LAST : LAST + 1, :] = jnp.maximum(upto - 1, 0)
    owner[SOME : SOME + 1, :] = jnp.max((down == lane).astype(jnp.int32), axis=0, keepdims=True)


def add_slots(owner, returned, runs, rows, width, orb_dev):
    total = jnp.zeros((runs.shape[1], width), jnp.float32)
    for t in range(runs.shape[0]):
        term = returned[owner[ORDER, t], rows, :width].astype(jnp.float32)
        total = term + jnp.where(owner[KEEP, t] > 0, total, 0.0)
        runs[t, :, :width] = total
    return [
        jnp.where(owner[SOME, o] > 0, runs[owner[LAST, o], :, :width], 0.0) for o in range(orb_dev)
    ]


def pair_kernel(
    n_row,
    n_col,
    slot,
    first,
    second,
    occ,
    energy_row,
    blocks_in,
    *refs,
):
    parts = len(PARTS)
    back = refs[:parts]
    part_sum, owner = refs[parts : parts + 2]
    (
        blocks,
        send_l,
        send_r,
        recv_l,
        recv_r,
        mat,
        weight,
        weight_t,
        table_v,
        energy_v,
        table,
        energy,
        asked,
        owner_v,
        runs,
        load_sem,
        ask_send,
        ask_recv,
        out_sem,
        in_sem,
        own_sem,
        sum_sem,
    ) = refs[parts + 2 :]
    row = lax.axis_index("row")
    col = lax.axis_index("col")
    orb_dev, virtuals, fitting = blocks.shape
    pairs = mat.shape[0]
    slots_f = n_row * I_CAP

    def to_row(e):
        return (row_step(row, e, 1), col)

    def to_col(e):
        return (row, col_step(col, e, 1))

    def from_row(e):
        return (row_step(row, e, -1), col)

    def from_col(e):
        return (row, col_step(col, e, -1))

    barrier = pltpu.get_barrier_semaphore()

    def greet(e, carry):
        pl.semaphore_signal(barrier, inc=1, device_id=to_col(e), device_id_type=MESH)

        @pl.when(e < n_row)
        def _():
            pl.semaphore_signal(barrier, inc=1, device_id=to_row(e), device_id_type=MESH)

        return carry

    lax.fori_loop(1, n_col, greet, 0)
    load = pltpu.make_async_copy(blocks_in, blocks, load_sem.at[0])
    load.start()
    plan(row, col, orb_dev, n_row, slot, first, second, occ, table_v, energy_v)
    to_scalar = (
        pltpu.make_async_copy(table_v, table, load_sem.at[1]),
        pltpu.make_async_copy(energy_v, energy, load_sem.at[2]),
    )
    for copy in to_scalar:
        copy.start()
    for copy in to_scalar:
        copy.wait()
    pl.semaphore_wait(barrier, n_row + n_col - 2)

    def ask_copy(place, target):
        return pltpu.make_async_remote_copy(
            src_ref=table.at[ASK],
            dst_ref=asked.at[place],
            send_sem=ask_send.at[place],
            recv_sem=ask_recv.at[place],
            device_id=target,
            device_id_type=MESH,
        )

    def ask(e, carry):
        ask_copy(n_row + e, from_col(e)).start()

        @pl.when(e < n_row)
        def _():
            ask_copy(e, from_row(e)).start()

        return carry

    lax.fori_loop(1, n_col, ask, 0)
    asked[0, 0] = table[ASK, 0]
    asked[n_row, n_row] = table[ASK, n_row]
    load.wait()

    def local_of(code):
        return jnp.where(code == NONE, 0, code)

    def copy_l(k, h, e):
        rows = pl.ds(h * PIECE, PIECE)
        place = pl.ds(e * I_CAP, I_CAP)
        return pltpu.make_async_remote_copy(
            src_ref=send_l[k].at[place, rows],
            dst_ref=recv_l[k].at[place, rows],
            send_sem=out_sem.at[0, k],
            recv_sem=in_sem.at[0, k],
            device_id=to_row(e),
            device_id_type=MESH,
        )

    def copy_r(k, h, e):
        rows = pl.ds(h * PIECE, PIECE)
        return pltpu.make_async_remote_copy(
            src_ref=send_r[k].at[e, rows],
            dst_ref=recv_r[k].at[e, rows],
            send_sem=out_sem.at[1, k],
            recv_sem=in_sem.at[1, k],
            device_id=to_col(e),
            device_id_type=MESH,
        )

    pieces = virtuals // PIECE
    for k, (start, width) in enumerate(PARTS):
        columns = slice(start, start + width)

        def forward(e, carry):
            if k == 0:
                ask_copy(n_row + e, from_col(e)).wait()
            send_r[k][e] = blocks[local_of(asked[n_row + e, n_row + e]), :, columns]
            copy_r(k, 0, e).start()

            @pl.when(e < n_row)
            def _():
                if k == 0:
                    ask_copy(e, from_row(e)).wait()
                code = asked[e, e]
                send_l[k][e * I_CAP] = blocks[local_of(code & 7), :, columns]
                send_l[k][e * I_CAP + 1] = blocks[local_of(code >> 3), :, columns]
                copy_l(k, 0, e).start()

            return carry

        lax.fori_loop(1, n_col, forward, 0)

        def forward_rest(e, carry):
            for h in range(1, pieces):
                copy_r(k, h, e).start()

                @pl.when(e < n_row)
                def _():
                    copy_l(k, h, e).start()

            return carry

        lax.fori_loop(1, n_col, forward_rest, 0)
        own = asked[0, 0]
        recv_l[k][0] = blocks[local_of(own & 7), :, columns]
        recv_l[k][1] = blocks[local_of(own >> 3), :, columns]
        recv_r[k][0] = blocks[local_of(asked[n_row, n_row]), :, columns]

    plan_owner(n_row, n_col, asked, owner_v)
    to_owner = pltpu.make_async_copy(owner_v, owner, load_sem.at[3])
    to_owner.start()

    virtual_row = jnp.broadcast_to(energy_row[...], (virtuals, virtuals))
    virtual_sum = virtual_row.T + virtual_row
    for k in range(parts):
        got_l = recv_l[k].at[pl.ds(I_CAP, slots_f - I_CAP)]
        got_r = recv_r[k].at[pl.ds(1, n_col - 1)]
        pltpu.make_async_copy(got_l, got_l, in_sem.at[0, k]).wait()
        pltpu.make_async_copy(got_r, got_r, in_sem.at[1, k]).wait()

        def integral(q, carry):
            left = recv_l[k][table[FS, q]]
            right = recv_r[k][table[SS, q]]
            found = lax.dot_general(
                left, right, (((1,), (1,)), ((), ())), preferred_element_type=jnp.float32
            )
            if k > 0:
                found = mat[q] + found
            if k < parts - 1:
                mat[q] = found
                return carry
            turned = found.T
            scale = 1.0 / (virtual_sum - energy[0, q])
            weight[q] = ((2.0 * found - turned) * scale).astype(jnp.bfloat16)
            weight_t[q] = ((2.0 * turned - found) * scale).astype(jnp.bfloat16)
            return carry

        lax.fori_loop(0, pairs, integral, 0, unroll=UNROLL)

    def back_l(k, h, e):
        rows = pl.ds(h * PIECE, PIECE)
        place = pl.ds(e * I_CAP, I_CAP)
        return pltpu.make_async_remote_copy(
            src_ref=send_l[k].at[place, rows],
            dst_ref=back[k].at[place, rows],
            send_sem=out_sem.at[2, k],
            recv_sem=in_sem.at[2, k],
            device_id=from_row(e),
            device_id_type=MESH,
        )

    def back_r(k, h, e):
        rows = pl.ds(h * PIECE, PIECE)
        return pltpu.make_async_remote_copy(
            src_ref=send_r[k].at[e, rows],
            dst_ref=back[k].at[slots_f + e, rows],
            send_sem=out_sem.at[3, k],
            recv_sem=in_sem.at[3, k],
            device_id=from_col(e),
            device_id_type=MESH,
        )

    def own_copies(k):
        own = pl.ds(0, I_CAP)
        return (
            pltpu.make_async_copy(send_l[k].at[own], back[k].at[own], own_sem.at[0, k]),
            pltpu.make_async_copy(send_r[k].at[0], back[k].at[slots_f], own_sem.at[1, k]),
        )

    def sent(k):
        return send_l[k].at[pl.ds(I_CAP, slots_f - I_CAP)], send_r[k].at[pl.ds(1, n_col - 1)]

    for k in BACK_ORDER:
        width = PARTS[k][1]
        sent_l, sent_r = sent(k)
        pltpu.make_async_copy(sent_l, sent_l, out_sem.at[0, k]).wait()
        pltpu.make_async_copy(sent_r, sent_r, out_sem.at[1, k]).wait()

        unroll = pairs if k == BACK_ORDER[0] else UNROLL

        def run(terms, table_row, n):
            before = mat[jnp.maximum(n * unroll - 1, 0), :, :width]
            for u, term in enumerate(terms):
                before = term + jnp.where(table[table_row, n * unroll + u] > 0, before, 0.0)
                mat[n * unroll + u, :, :width] = before

        def left_terms(n, carry):
            terms = []
            for u in range(unroll):
                right = recv_r[k][table[SS, n * unroll + u]]
                terms.append(jnp.dot(weight[n * unroll + u], right, preferred_element_type=jnp.float32))
            run(terms, KF, n)
            return carry

        def right_terms(n, carry):
            terms = []
            for u in range(unroll):
                q = table[OS, n * unroll + u]
                left = recv_l[k][table[FS, q]]
                terms.append(jnp.dot(weight_t[q], left, preferred_element_type=jnp.float32))
            run(terms, KS, n)
            return carry

        def left_out(e, carry):
            for s in range(I_CAP):
                sums = mat[table[LF, e * I_CAP + s], :, :width]
                send_l[k][e * I_CAP + s] = sums.astype(jnp.bfloat16)
            return carry

        def right_out(e, carry):
            send_r[k][e] = mat[table[LS, e], :, :width].astype(jnp.bfloat16)
            return carry

        def send_right(e, carry):
            for h in range(pieces):
                back_r(k, h, e).start()
            return carry

        def send_left(e, carry):
            for h in range(pieces):
                back_l(k, h, e).start()
            return carry

        def send_both(h):
            def send(e, carry):
                back_r(k, h, e).start()

                @pl.when(e < n_row)
                def _():
                    back_l(k, h, e).start()

                return carry

            return send

        lax.fori_loop(0, pairs // unroll, right_terms, 0)
        lax.fori_loop(0, n_col, right_out, 0)
        if k == BACK_ORDER[0]:
            lax.fori_loop(1, n_col, send_right, 0)
        lax.fori_loop(0, pairs // unroll, left_terms, 0)
        lax.fori_loop(0, n_row, left_out, 0)
        if k == BACK_ORDER[0]:
            lax.fori_loop(1, n_row, send_left, 0)
        else:
            for h in range(pieces):
                lax.fori_loop(1, n_col, send_both(h), 0)
        for copy in own_copies(k):
            copy.start()

    def returned(k):
        for copy in own_copies(k):
            copy.wait()
        got_l = back[k].at[pl.ds(I_CAP, slots_f - I_CAP)]
        got_r = back[k].at[pl.ds(slots_f + 1, n_col - 1)]
        pltpu.make_async_copy(got_l, got_l, in_sem.at[2, k]).wait()
        pltpu.make_async_copy(got_r, got_r, in_sem.at[3, k]).wait()

    def store(n, k):
        start, width = PARTS[k]
        return pltpu.make_async_copy(
            mat.at[pl.ds(n % 2 * orb_dev, orb_dev), :, pl.ds(0, width)],
            part_sum.at[:, :, pl.ds(start, width)],
            sum_sem.at[1, n],
        )

    to_owner.wait()
    for n, k in enumerate(BACK_ORDER[:-1]):
        width = PARTS[k][1]
        stage = weight.at[:, :, pl.ds(0, width)]
        returned(k)
        fetch = pltpu.make_async_copy(back[k], stage, sum_sem.at[0, n])
        fetch.start()
        if n >= 2:
            store(n - 2, BACK_ORDER[n - 2]).wait()
        fetch.wait()

        def add_up(t, carry):
            rows = pl.ds(pl.multiple_of(t * SUM_ROWS, SUM_ROWS), SUM_ROWS)
            for o, total in enumerate(add_slots(owner, weight, runs, rows, width, orb_dev)):
                mat[n % 2 * orb_dev + o, rows, :width] = total
            return carry

        lax.fori_loop(0, virtuals // SUM_ROWS, add_up, 0)
        store(n, k).start()

    returned(BACK_ORDER[-1])
    for n in range(max(parts - 3, 0), parts - 1):
        store(n, BACK_ORDER[n]).wait()
    for k in BACK_ORDER:
        sent_l, sent_r = sent(k)
        pltpu.make_async_copy(sent_l, sent_l, out_sem.at[2, k]).wait()
        pltpu.make_async_copy(sent_r, sent_r, out_sem.at[3, k]).wait()


def sum_kernel(owner, part_sum, back, out, runs):
    orb_dev, rows, _ = out.shape
    start, width = PARTS[BACK_ORDER[-1]]
    for r in range(0, rows, SUM_ROWS):
        part = pl.ds(r, SUM_ROWS)
        for o, total in enumerate(add_slots(owner, back, runs, part, width, orb_dev)):
            out[o, part, start : start + width] = total
    out[:, :, :start] = part_sum[...]


def shards(orbital_blocks, orbital_slot, pair_first, pair_second, occupied_energy, virtual_energy):
    n_row = lax.axis_size("row")
    n_col = lax.axis_size("col")
    orb_dev, virtuals, fitting = orbital_blocks.shape
    pairs = pair_first.shape[0]
    parts = len(PARTS)
    slots_f = n_row * I_CAP
    slots = slots_f + n_col
    summed = PARTS[BACK_ORDER[-1]][0]
    smem = pl.BlockSpec(memory_space=pltpu.SMEM)
    vmem = pl.BlockSpec(memory_space=pltpu.VMEM)
    hbm = pl.BlockSpec(memory_space=pl.ANY)

    def buffers(count):
        return [pltpu.VMEM((count, virtuals, width), jnp.bfloat16) for _, width in PARTS]

    *back, part_sum, owner = pl.pallas_call(
        functools.partial(pair_kernel, n_row, n_col),
        out_shape=(
            *[jax.ShapeDtypeStruct((slots, virtuals, width), jnp.bfloat16) for _, width in PARTS],
            jax.ShapeDtypeStruct((orb_dev, virtuals, summed), jnp.float32),
            jax.ShapeDtypeStruct((8, 128), jnp.int32),
        ),
        in_specs=[smem, smem, smem, smem, vmem, hbm],
        out_specs=(hbm,) * (parts + 1) + (smem,),
        scratch_shapes=[
            pltpu.VMEM((orb_dev, virtuals, fitting), jnp.bfloat16),
            buffers(slots_f),
            buffers(n_col),
            buffers(slots_f),
            buffers(n_col),
            pltpu.VMEM((pairs, virtuals, virtuals), jnp.float32),
            pltpu.VMEM((pairs, virtuals, virtuals), jnp.bfloat16),
            pltpu.VMEM((pairs, virtuals, virtuals), jnp.bfloat16),
            pltpu.VMEM((8, 128), jnp.int32),
            pltpu.VMEM((8, 128), jnp.float32),
            pltpu.SMEM((8, 128), jnp.int32),
            pltpu.SMEM((8, 128), jnp.float32),
            pltpu.SMEM((n_row + n_col, 128), jnp.int32),
            pltpu.VMEM((8, 128), jnp.int32),
            pltpu.VMEM((slots, SUM_ROWS, 256), jnp.float32),
            pltpu.SemaphoreType.DMA((4,)),
            pltpu.SemaphoreType.DMA((n_row + n_col,)),
            pltpu.SemaphoreType.DMA((n_row + n_col,)),
            pltpu.SemaphoreType.DMA((4, parts)),
            pltpu.SemaphoreType.DMA((4, parts)),
            pltpu.SemaphoreType.DMA((2, parts)),
            pltpu.SemaphoreType.DMA((2, parts)),
        ],
        compiler_params=pltpu.CompilerParams(
            collective_id=0, has_side_effects=True, vmem_limit_bytes=60 * 2**20
        ),
    )(
        orbital_slot,
        pair_first,
        pair_second,
        occupied_energy,
        virtual_energy.reshape(1, virtuals),
        orbital_blocks,
    )

    rows = ROWS
    width = PARTS[BACK_ORDER[-1]][1]
    return pl.pallas_call(
        sum_kernel,
        grid=(virtuals // rows,),
        out_shape=jax.ShapeDtypeStruct(orbital_blocks.shape, jnp.float32),
        in_specs=[
            smem,
            pl.BlockSpec((orb_dev, rows, summed), lambda i: (0, i, 0)),
            pl.BlockSpec((slots, rows, width), lambda i: (0, i, 0)),
        ],
        out_specs=pl.BlockSpec((orb_dev, rows, fitting), lambda i: (0, i, 0)),
        scratch_shapes=[pltpu.VMEM((slots, SUM_ROWS, width), jnp.float32)],
        compiler_params=pltpu.CompilerParams(vmem_limit_bytes=60 * 2**20),
    )(owner, part_sum, back[BACK_ORDER[-1]])


def solution(mesh):
    return jax.shard_map(
        shards,
        mesh=mesh,
        in_specs=(
            P(("row", "col"), None, None),
            P(),
            P(("row", "col")),
            P(("row", "col")),
            P(),
            P(),
        ),
        out_specs=P(("row", "col"), None, None),
        check_vma=False,
    )
```
